32 devices in a mesh: seq: 8 (over y, x, core), tp: 4 (over z).
Axes of the slice: x: 2, y: 2, z: 4, core: 2. Of those that a mesh axis runs over, the one named last changes fastest.
Arguments:
- targets: bfloat16 [8192, 2048], P('seq', 'tp'), may hold values from -6 to 6
- w_query: bfloat16 [2048, 1024], P(None, 'tp'), may hold values from -0.125 to 0.125
- w_gate: bfloat16 [2048, 1024], P(None, 'tp'), may hold values from -0.125 to 0.125
- norm_gain: float32 [1024], P('tp'), may hold values from 0.25 to 1.75
- hist_keys: bfloat16 [8192, 1024], P('seq', 'tp'), may hold values from -6 to 6
- hist_values: bfloat16 [8192, 1024], P('seq', 'tp')
- user_offset: int32 [128], P('seq'), may hold values from 0 to 8191, as said below
- user_length: int32 [128], P('seq'), may hold values from 16 to 2048
- target_user: int32 [8192], P('seq'), may hold values from 0 to 127, as said below
Outputs:
- scored: bfloat16 [8192, 1024], P('seq', 'tp')
The draws below stay inside these ranges and needn't reach their ends.
Inputs may be any that keep to these rules, and one draw needn't show every extreme that they name: `user_offset`: the users of seq index i are users i * 16 to (i + 1) * 16 - 1; each such user's offset lies in history positions i * 1024 to (i + 1) * 1024 - 1. A history may run past position 8191 and continue at position 0. `target_user`: target items of seq index i belong to users of seq index i.
All inputs are finite; a program needn't handle non-finite values.
Results may differ from the reference program's by a relative error of at most 0.0058.
Values may be sent and summed in bfloat16 or wider, within the bound.
A program may use at most 64 MiB of HBM per device.

```python
import math
import jax
import jax.numpy as jnp
from jax import lax

D = 2048
HEADS = 8
HDIM = 128
SPAN = 2
U_DEV = 16
TGT_DEV = 1024
HIST_DEV = 1024
HQ = 1024
TARGETS = 8192
HIST = 8192
USERS = 128
MAXLEN = 2048
MINLEN = 16
N_SEQ = 8


def draw_hist_values(key, part):
    first, second = jax.random.split(key)
    columns = jnp.exp(jax.random.uniform(first, (1, HQ), jnp.float32, 0.0, math.log(10.0)))
    base = jax.random.normal(second, (HIST, HQ), jnp.float32)
    return (base * columns).astype(jnp.bfloat16)


def draw_user_offset(key, part):
    owner = jnp.arange(USERS, dtype=jnp.int32) // U_DEV
    local = jax.random.randint(jax.random.fold_in(key, 11), (USERS,), 0, HIST_DEV, dtype=jnp.int32)
    offsets = owner * HIST_DEV + local
    return offsets.at[USERS - 1].set(HIST - 1)


def draw_user_length(key, part):
    kinds = jax.random.randint(jax.random.fold_in(key, 21), (USERS // U_DEV,), 0, 3, dtype=jnp.int32)
    capped = jnp.where(kinds == 0, max(HIST_DEV // 8, MINLEN), jnp.where(kinds == 1, HIST_DEV, MAXLEN))
    capped = jnp.repeat(capped, U_DEV)
    extra = jax.random.randint(jax.random.fold_in(key, 22), (USERS,), 0, capped - MINLEN + 1, dtype=jnp.int32)
    lengths = MINLEN + extra
    lengths = lengths.at[USERS - 1].set(MAXLEN)
    return lengths.at[USERS - 2].set(MINLEN)


def draw_target_user(key, part):
    places = jnp.arange(TARGETS, dtype=jnp.int32)
    owner = places // TGT_DEV
    local = jax.random.randint(jax.random.fold_in(key, 31), (TARGETS,), 0, U_DEV, dtype=jnp.int32)
    local = jnp.where(places % TGT_DEV == 0, U_DEV - 1, local)
    local = jnp.where(places % TGT_DEV == 1, 0, local)
    return owner * U_DEV + local


def levels(stream_key, extent, cuts, least, high):
    factor_of, own = 1.0, jax.random.fold_in(stream_key, 6)
    for position, shards_of in cuts:
        steps = jnp.exp(jax.random.uniform(jax.random.fold_in(own, position), (shards_of,), jnp.float32, least / len(cuts), high / len(cuts)))
        factor_of = factor_of * jnp.repeat(steps, extent[position] // shards_of).reshape([-1 if axis == position else 1 for axis in range(len(extent))])
    return factor_of


def scatter_about(stream_key, dims, scale, reach, shards=(), kind=jnp.bfloat16):
    factor_of = levels(stream_key, dims, shards, -0.22, 0.18) if shards else 1.0
    drawn = jax.random.normal(stream_key, dims, jnp.float32) * scale * factor_of
    return jnp.minimum(jnp.maximum(drawn, -reach), reach).astype(kind)


def setup_inputs(seed: int = 0) -> dict:
    splits = jax.random.split(jax.random.key(seed), 10)
    return {
        "targets": scatter_about(splits[0], (TARGETS, D), 1.0, 6.0, ((0, 8), (1, 4))),
        "w_query": scatter_about(splits[1], (D, HQ), D ** -0.5, 0.125, ((1, 4),)),
        "w_gate": scatter_about(splits[2], (D, HQ), D ** -0.5, 0.125, ((1, 4),)),
        "norm_gain": jnp.clip(1.0 + 0.15 * jax.random.normal(splits[3], (HQ,), jnp.float32), 0.25, 1.75),
        "hist_keys": scatter_about(splits[4], (HIST, HQ), 1.0, 6.0, ((0, 8), (1, 4))),
        "hist_values": draw_hist_values(jax.random.fold_in(splits[9], 71), 0),
        "user_offset": draw_user_offset(jax.random.fold_in(splits[9], 71), 0),
        "user_length": draw_user_length(jax.random.fold_in(splits[9], 71), 0),
        "target_user": draw_target_user(jax.random.fold_in(splits[9], 71), 0),
    }


def reference(targets, w_query, w_gate, norm_gain, hist_keys, hist_values, user_offset, user_length, target_user):
    width = SPAN * HIST_DEV
    ext_keys = jnp.concatenate([hist_keys, hist_keys[:width]], axis=0)
    ext_values = jnp.concatenate([hist_values, hist_values[:width]], axis=0)
    window = (SPAN + 1) * HIST_DEV
    scale = HDIM ** (-0.5)

    def one_block(index):
        index = index.astype(jnp.int32)
        tstart = (index * TGT_DEV).astype(jnp.int32)
        hstart = (index * HIST_DEV).astype(jnp.int32)
        rows = lax.dynamic_slice_in_dim(targets, tstart, TGT_DEV, 0)
        users = lax.dynamic_slice_in_dim(target_user, tstart, TGT_DEV, 0)
        query = jnp.dot(rows, w_query, preferred_element_type=jnp.float32).astype(jnp.bfloat16)
        gate = jax.nn.silu(jnp.dot(rows, w_gate, preferred_element_type=jnp.float32))
        offsets = user_offset[users]
        lengths = user_length[users]
        keys = lax.dynamic_slice_in_dim(ext_keys, hstart, window, 0)
        values = lax.dynamic_slice_in_dim(ext_values, hstart, window, 0)
        places = (hstart + jnp.arange(window, dtype=jnp.int32)) % HIST
        relative = (places[None, :] - offsets[:, None]) % HIST
        inside = relative < lengths[:, None]
        qheads = query.astype(jnp.float32).reshape(TGT_DEV, HEADS, HDIM)
        kheads = keys.astype(jnp.float32).reshape(window, HEADS, HDIM)
        vheads = values.astype(jnp.float32).reshape(window, HEADS, HDIM)
        scores = jnp.einsum('thd,phd->thp', qheads, kheads) * scale
        weight = jnp.where(inside[:, None, :], jax.nn.silu(scores), 0.0).astype(jnp.bfloat16)
        attended = jnp.einsum('thp,phd->thd', weight.astype(jnp.float32), vheads).reshape(TGT_DEV, HQ)
        mean = lax.optimization_barrier(jnp.sum(attended, axis=1, keepdims=True)) / HQ
        var = lax.optimization_barrier(jnp.sum(attended * attended, axis=1, keepdims=True)) / HQ - mean * mean
        normed = (attended - mean) / jnp.sqrt(var + 1e-05)
        return (normed * norm_gain[None, :] * gate).astype(jnp.bfloat16)
    blocks = lax.map(one_block, jnp.arange(N_SEQ, dtype=jnp.int32))
    return blocks.reshape(TARGETS, HQ)
```

```python
import functools

import jax
import jax.numpy as jnp
from jax import lax
from jax.experimental import pallas as pl
from jax.experimental.pallas import tpu as pltpu
from jax.sharding import PartitionSpec as P

HDIM = 128
SPAN = 2
HQ = 1024
R = 128
BLOCK = 512
AHEAD = 2
LAG = 3
GROUP = 8
MESH = pl.DeviceIdType.MESH


def kernel(
    n_seq,
    targets,
    w_query,
    w_gate,
    gain,
    hist_keys,
    hist_values,
    user_offset,
    user_length,
    target_user,
    out,
    pieces,
    w_own,
    w_outer,
    kv,
    qg,
    qg_outer,
    gate,
    att,
    mids,
    halves,
    stats,
    load_sem,
    piece_send,
    piece_recv,
    w_send,
    w_recv,
    kv_send,
    kv_recv,
    qg_send,
    qg_recv,
    stat_send,
    stat_recv,
):
    rows_total, width = targets.shape
    local = w_query.shape[1]
    heads = local // HDIM
    hist_rows = hist_keys.shape[0]
    users = user_offset.shape[0]
    chunks = rows_total // R
    s = lax.axis_index("seq")
    t = lax.axis_index("tp")
    inner = (t == 1) | (t == 2)
    outer = (t == 0) | (t == 3)
    out_of = 3 * (t - 1)
    across = 3 - t
    in_of = 1 + t // 3
    behind = lax.rem(s + n_seq - 1, n_seq)
    ahead = lax.rem(s + 1, n_seq)
    place = lax.rem(s, GROUP)
    base = s - place
    pair = place // 2
    core = lax.rem(place, 2)
    sibling = base + place + 1 - 2 * core
    w_rows = w_query.shape[0] // GROUP

    def rows(c):
        return pl.ds(pl.multiple_of(c * R, R), R)

    def remote(src, dst, send, recv, device):
        return pltpu.make_async_remote_copy(
            src_ref=src, dst_ref=dst, send_sem=send, recv_sem=recv, device_id=device, device_id_type=MESH
        )

    def piece(c, origin, to, which):
        ref = pieces.at[origin, rows(c)]
        return remote(ref, ref, piece_send.at[c, which], piece_recv.at[c, origin], (s, to))

    def w_slice(buffer, j):
        return buffer.at[:, pl.ds(pl.multiple_of(j * w_rows, w_rows), w_rows)]

    def w_copy(src, j, which, device):
        return remote(w_slice(src, j), w_slice(w_outer, j), w_send.at[which], w_recv.at[j], device)

    def peer_place(k):
        return lax.rem(pair + k, GROUP // 2) * 2 + core

    def kv_copy(hop, which):
        return remote(
            kv.at[hop, which], kv.at[hop + 1, which], kv_send.at[hop, which], kv_recv.at[hop, which], (behind, t)
        )

    def qg_copy(c, which, to):
        return remote(
            qg_outer.at[which, rows(c)], qg.at[which, rows(c)], qg_send.at[c, which], qg_recv.at[c, which], (s, to)
        )

    def stat_copy(c, k):
        peer = lax.rem(t + k, 4)
        return remote(stats.at[t, c], stats.at[t, c], stat_send.at[c, k], stat_recv.at[c, t], (s, peer))

    def stat_arrival(c, k):
        peer = lax.rem(t + k, 4)
        return remote(stats.at[peer, c], stats.at[peer, c], stat_send.at[c, k], stat_recv.at[c, peer], (s, peer))

    loads = [
        pltpu.make_async_copy(src, dst, load_sem.at[i])
        for i, (src, dst) in enumerate(
            [
                (targets, pieces.at[t]),
                (hist_keys, kv.at[0, 0]),
                (hist_values, kv.at[0, 1]),
                (w_query, w_own.at[0]),
                (w_gate, w_own.at[1]),
            ]
        )
    ]
    for load in loads:
        load.start()

    barrier = pltpu.get_barrier_semaphore()
    partners = [(s, lax.rem(t + k, 4)) for k in (1, 2, 3)]
    partners += [(behind, t), (ahead, t)]
    partners += [(base + peer_place(k), t) for k in (1, 2, 3)]
    partners += [(sibling, t)]
    for device in partners:
        pl.semaphore_signal(barrier, inc=1, device_id=device, device_id_type=MESH)
    pl.semaphore_wait(barrier, len(partners))

    for load in loads:
        load.wait()

    @pl.when(outer)
    def _():
        piece(0, t, in_of, 0).start()
        w_copy(w_own, place, 0, (s, in_of)).start()

    @pl.when(inner)
    def _():
        for c in range(AHEAD):
            piece(c, t, across, 0).start()

    for which in range(2):
        kv_copy(0, which).start()

    mine = target_user[...] - s * users
    start_of = jnp.zeros(mine.shape, jnp.float32)
    length_of = jnp.zeros(mine.shape, jnp.float32)
    for u in range(users):
        match = mine == u
        start_of = jnp.where(match, (user_offset[u] - s * hist_rows).astype(jnp.float32), start_of)
        length_of = jnp.where(match, user_length[u].astype(jnp.float32), length_of)
    half_of = (length_of - 1.0) * 0.5
    mid_of = start_of + half_of
    for c in range(chunks):
        mids[c * R : (c + 1) * R, :] = jnp.broadcast_to(mid_of[c : c + 1, :], (R, R)).T
        halves[c * R : (c + 1) * R, :] = jnp.broadcast_to(half_of[c : c + 1, :], (R, R)).T

    def project(c, weights):
        sums = [jnp.zeros((R, local), jnp.float32)] * 2
        for o in range(4):
            x = pieces[o, rows(c)]
            for i in range(2):
                sums[i] = sums[i] + jnp.dot(
                    x, weights[i, o * width : (o + 1) * width, :], preferred_element_type=jnp.float32
                )
        half = sums[1] * 0.5
        return sums[0].astype(jnp.bfloat16), half + half * jnp.tanh(half)

    def attend(c, _):
        query = qg[0, rows(c)]
        repeat = BLOCK // R
        mid = jnp.concatenate([mids[rows(c)]] * repeat, axis=1)
        half_width = jnp.concatenate([halves[rows(c)]] * repeat, axis=1)
        lanes = lax.broadcasted_iota(jnp.int32, (1, BLOCK), 1)

        def hop_step(hop, sums):
            sums = list(sums)
            for b in range(hist_rows // BLOCK):
                places = (lanes + (hop * hist_rows + b * BLOCK)).astype(jnp.float32)
                inside = jnp.abs(places - mid) <= half_width
                for h in range(heads):
                    cols = slice(h * HDIM, (h + 1) * HDIM)
                    keys = kv[hop, 0, b * BLOCK : (b + 1) * BLOCK, cols]
                    values = kv[hop, 1, b * BLOCK : (b + 1) * BLOCK, cols]
                    score = lax.dot_general(
                        query[:, cols], keys, (((1,), (1,)), ((), ())), preferred_element_type=jnp.float32
                    )
                    x = score * (0.5 * HDIM**-0.5)
                    weight = jnp.where(inside, x + x * jnp.tanh(x), 0.0).astype(jnp.bfloat16)
                    sums[h] = sums[h] + jnp.dot(weight, values, preferred_element_type=jnp.float32)
            return tuple(sums)

        sums = lax.fori_loop(0, SPAN + 1, hop_step, (jnp.zeros((R, HDIM), jnp.float32),) * heads)
        attended = jnp.concatenate(sums, axis=1)
        att[rows(c)] = attended
        first = jnp.sum(attended, axis=1, keepdims=True)
        second = jnp.sum(attended * attended, axis=1, keepdims=True)
        lane = lax.broadcasted_iota(jnp.int32, (R, R), 1)
        both = jnp.where(lane == 0, first, jnp.where(lane == 1, second, 0.0))
        stats[t, c] = both.T[:8]
        for k in (1, 2, 3):
            stat_copy(c, k).start()
        return 0

    @pl.when(outer)
    def _():
        piece(1, t, in_of, 0).start()

        def send_step(c, _):
            piece(c - AHEAD, t, in_of, 0).wait_send()
            piece(c, t, in_of, 0).start()
            return 0

        lax.fori_loop(AHEAD, chunks // 2, send_step, 0)
        for which in range(2):
            kv_copy(0, which).wait_recv()
            kv_copy(1, which).start()
        lax.fori_loop(chunks // 2, chunks, send_step, 0)
        for c in range(chunks - AHEAD, chunks):
            piece(c, t, in_of, 0).wait_send()
        w_copy(w_own, place, 0, (s, in_of)).wait_send()
        for which in range(2):
            kv_copy(1, which).wait_recv()

        def outer_step(c, _):
            for which in range(2):
                qg_copy(c, which, in_of).wait_recv()
            gate[rows(c)] = qg[1, rows(c)].astype(jnp.float32)
            return attend(c, 0)

        lax.fori_loop(0, chunks, outer_step, 0)

    @pl.when(inner)
    def _():
        for c in range(AHEAD):
            piece(c, out_of, across, 1).wait_recv()
            piece(c, out_of, across, 1).start()
        w_copy(w_outer, place, 0, (s, t)).wait_recv()
        for k in (1, 2, 3):
            w_copy(w_outer, place, k, (base + peer_place(k), t)).start()
        w_copy(w_outer, place, 4, (sibling, t)).start()

        def project_outer(c, _):
            query, gated = project(c, w_outer)
            qg_outer[0, rows(c)] = query
            qg_outer[1, rows(c)] = gated.astype(jnp.bfloat16)
            for which in range(2):
                qg_copy(c, which, out_of).start()
            return 0

        def inner_step(c, _):
            @pl.when(c + AHEAD < chunks)
            def _():
                piece(c + AHEAD, t, across, 0).start()
                piece(c + AHEAD, out_of, across, 1).wait_recv()
                piece(c + AHEAD, out_of, across, 1).start()

            @pl.when(c == 1)
            def _():
                for which in range(2):
                    kv_copy(0, which).wait_recv()
                    kv_copy(1, which).start()
                for k in (1, 2, 3):
                    w_copy(w_outer, peer_place(k), k, (sibling, t)).wait_recv()
                    w_copy(w_outer, peer_place(k), 4 + k, (sibling, t)).start()

            @pl.when(c == LAG)
            def _():
                for k in range(GROUP // 2):
                    w_copy(w_outer, peer_place(k) + 1 - 2 * core, 4 + k, (sibling, t)).wait_recv()
                for which in range(2):
                    kv_copy(1, which).wait_recv()

            piece(c, across, across, 0).wait_recv()
            piece(c, 3 - out_of, across, 0).wait_recv()
            lax.fori_loop(jnp.where(c <= LAG, 0, c), jnp.where(c < LAG, 0, c + 1), project_outer, 0)
            query, gated = project(c, w_own)
            qg[0, rows(c)] = query
            gate[rows(c)] = gated
            done_before = jnp.minimum(jnp.maximum(2 * (c - LAG), 0), c)
            done_after = jnp.minimum(jnp.maximum(2 * (c - LAG + 1), 0), c + 1)
            lax.fori_loop(done_before, done_after, attend, 0)
            return 0

        lax.fori_loop(0, chunks, inner_step, 0)

    def finish(c, _):
        total = stats[t, c]
        for k in (1, 2, 3):
            stat_arrival(c, k).wait_recv()
            total = total + stats[lax.rem(t + k, 4), c]
        columns = jnp.concatenate([total, jnp.zeros((R - 8, R), jnp.float32)], axis=0).T
        mean = columns[:, 0:1] * (1.0 / HQ)
        var = columns[:, 1:2] * (1.0 / HQ) - mean * mean
        normed = (att[rows(c)] - mean) * lax.rsqrt(var + 1e-05)
        out[rows(c)] = (normed * gain[...] * gate[rows(c)]).astype(jnp.bfloat16)
        return 0

    lax.fori_loop(0, chunks, finish, 0)

    for hop in range(SPAN):
        for which in range(2):
            kv_copy(hop, which).wait_send()

    def close_stats(c, _):
        for k in (1, 2, 3):
            stat_copy(c, k).wait_send()
        return 0

    lax.fori_loop(0, chunks, close_stats, 0)

    @pl.when(inner)
    def _():
        def close(c, _):
            piece(c, t, across, 0).wait_send()
            piece(c, out_of, across, 1).wait_send()
            for which in range(2):
                qg_copy(c, which, out_of).wait_send()
            return 0

        lax.fori_loop(0, chunks, close, 0)
        for k in (1, 2, 3):
            w_copy(w_outer, place, k, (base + peer_place(k), t)).wait_send()
        for k in range(GROUP // 2):
            w_copy(w_outer, peer_place(k), 4 + k, (sibling, t)).wait_send()


def body(
    n_seq, targets, w_query, w_gate, norm_gain, hist_keys, hist_values, user_offset, user_length, target_user
):
    rows_total, width = targets.shape
    depth, local = w_query.shape
    hist_rows = hist_keys.shape[0]
    chunks = rows_total // R
    anywhere = pl.BlockSpec(memory_space=pl.ANY)
    vmem = pl.BlockSpec(memory_space=pltpu.VMEM)
    smem = pl.BlockSpec(memory_space=pltpu.SMEM)
    dma = pltpu.SemaphoreType.DMA
    bf16, f32 = jnp.bfloat16, jnp.float32
    flops = 4 * rows_total * (1.5 * depth * local + (SPAN + 1) * hist_rows * local)
    return pl.pallas_call(
        functools.partial(kernel, n_seq),
        out_shape=jax.ShapeDtypeStruct((rows_total, local), bf16),
        in_specs=[anywhere, anywhere, anywhere, vmem, anywhere, anywhere, smem, smem, vmem],
        out_specs=vmem,
        scratch_shapes=[
            pltpu.VMEM((4, rows_total, width), bf16),
            pltpu.VMEM((2, depth, local), bf16),
            pltpu.VMEM((2, depth, local), bf16),
            pltpu.VMEM((SPAN + 1, 2, hist_rows, local), bf16),
            pltpu.VMEM((2, rows_total, local), bf16),
            pltpu.VMEM((2, rows_total, local), bf16),
            pltpu.VMEM((rows_total, local), f32),
            pltpu.VMEM((rows_total, local), f32),
            pltpu.VMEM((rows_total, R), f32),
            pltpu.VMEM((rows_total, R), f32),
            pltpu.VMEM((4, chunks, 8, R), f32),
            dma((5,)),
            dma((chunks, 2)),
            dma((chunks, 4)),
            dma((8,)),
            dma((GROUP,)),
            dma((SPAN, 2)),
            dma((SPAN, 2)),
            dma((chunks, 2)),
            dma((chunks, 2)),
            dma((chunks, 4)),
            dma((chunks, 4)),
        ],
        compiler_params=pltpu.CompilerParams(
            collective_id=0, has_side_effects=True, vmem_limit_bytes=48 * 1024 * 1024
        ),
        cost_estimate=pl.CostEstimate(flops=int(flops), bytes_accessed=5 * 1024 * 1024, transcendentals=0),
    )(
        targets,
        w_query,
        w_gate,
        norm_gain.reshape(1, local),
        hist_keys,
        hist_values,
        user_offset,
        user_length,
        target_user.reshape(chunks, R),
    )


def solution(mesh):
    return jax.shard_map(
        functools.partial(body, mesh.shape["seq"]),
        mesh=mesh,
        in_specs=(
            P("seq", "tp"),
            P(None, "tp"),
            P(None, "tp"),
            P("tp"),
            P("seq", "tp"),
            P("seq", "tp"),
            P("seq"),
            P("seq"),
            P("seq"),
        ),
        out_specs=P("seq", "tp"),
        check_vma=False,
    )
```

```python
import functools

import jax
import jax.numpy as jnp
from jax import lax
from jax.experimental import pallas as pl
from jax.experimental.pallas import tpu as pltpu
from jax.sharding import PartitionSpec as P

HDIM = 128
SPAN = 2
HQ = 1024
R = 128
BLOCK = 256
AHEAD = 2
LAG = 2
GROUP = 8
MESH = pl.DeviceIdType.MESH


def kernel(
    n_seq,
    targets,
    w_query,
    w_gate,
    gain,
    hist_keys,
    hist_values,
    user_offset,
    user_length,
    target_user,
    out,
    pieces,
    w_own,
    w_outer,
    kv,
    qg,
    qg_outer,
    gate,
    att,
    mids,
    halves,
    stats,
    load_sem,
    piece_send,
    piece_recv,
    w_send,
    w_recv,
    kv_send,
    kv_recv,
    qg_send,
    qg_recv,
    stat_send,
    stat_recv,
):
    rows_total, width = targets.shape
    local = w_query.shape[1]
    heads = local // HDIM
    hist_rows = hist_keys.shape[0]
    users = user_offset.shape[0]
    chunks = rows_total // R
    s = lax.axis_index("seq")
    t = lax.axis_index("tp")
    inner = (t == 1) | (t == 2)
    outer = (t == 0) | (t == 3)
    out_of = 3 * (t - 1)
    across = 3 - t
    in_of = 1 + t // 3
    behind = lax.rem(s + n_seq - 1, n_seq)
    ahead = lax.rem(s + 1, n_seq)
    place = lax.rem(s, GROUP)
    base = s - place
    pair = place // 2
    core = lax.rem(place, 2)
    sibling = base + place + 1 - 2 * core
    w_rows = w_query.shape[0] // GROUP

    def rows(c):
        return pl.ds(pl.multiple_of(c * R, R), R)

    def remote(src, dst, send, recv, device):
        return pltpu.make_async_remote_copy(
            src_ref=src, dst_ref=dst, send_sem=send, recv_sem=recv, device_id=device, device_id_type=MESH
        )

    def piece(c, origin, to, which):
        ref = pieces.at[origin, rows(c)]
        return remote(ref, ref, piece_send.at[c, which], piece_recv.at[c, origin], (s, to))

    def w_slice(buffer, j):
        return buffer.at[:, pl.ds(pl.multiple_of(j * w_rows, w_rows), w_rows)]

    def w_copy(src, j, which, device):
        return remote(w_slice(src, j), w_slice(w_outer, j), w_send.at[which], w_recv.at[j], device)

    def peer_place(k):
        return lax.rem(pair + k, GROUP // 2) * 2 + core

    def kv_copy(hop, which):
        return remote(
            kv.at[hop, which], kv.at[hop + 1, which], kv_send.at[hop, which], kv_recv.at[hop, which], (behind, t)
        )

    def qg_copy(c, which, to):
        return remote(
            qg_outer.at[which, rows(c)], qg.at[which, rows(c)], qg_send.at[c, which], qg_recv.at[c, which], (s, to)
        )

    def stat_copy(c, k):
        peer = lax.rem(t + k, 4)
        return remote(stats.at[t, c], stats.at[t, c], stat_send.at[c, k], stat_recv.at[c, t], (s, peer))

    def stat_arrival(c, k):
        peer = lax.rem(t + k, 4)
        return remote(stats.at[peer, c], stats.at[peer, c], stat_send.at[c, k], stat_recv.at[c, peer], (s, peer))

    loads = [
        pltpu.make_async_copy(src, dst, load_sem.at[i])
        for i, (src, dst) in enumerate(
            [
                (targets, pieces.at[t]),
                (hist_keys, kv.at[0, 0]),
                (hist_values, kv.at[0, 1]),
                (w_query, w_own.at[0]),
                (w_gate, w_own.at[1]),
            ]
        )
    ]
    for load in loads:
        load.start()

    barrier = pltpu.get_barrier_semaphore()
    partners = [(s, lax.rem(t + k, 4)) for k in (1, 2, 3)]
    partners += [(behind, t), (ahead, t)]
    partners += [(base + peer_place(k), t) for k in (1, 2, 3)]
    partners += [(sibling, t)]
    for device in partners:
        pl.semaphore_signal(barrier, inc=1, device_id=device, device_id_type=MESH)
    pl.semaphore_wait(barrier, len(partners))

    for load in loads:
        load.wait()

    @pl.when(outer)
    def _():
        piece(0, t, in_of, 0).start()
        w_copy(w_own, place, 0, (s, in_of)).start()

    @pl.when(inner)
    def _():
        for c in range(AHEAD):
            piece(c, t, across, 0).start()

    for which in range(2):
        kv_copy(0, which).start()

    att[...] = jnp.zeros(att.shape, jnp.float32)

    mine = target_user[...] - s * users
    start_of = jnp.zeros(mine.shape, jnp.float32)
    length_of = jnp.zeros(mine.shape, jnp.float32)
    for u in range(users):
        match = mine == u
        start_of = jnp.where(match, (user_offset[u] - s * hist_rows).astype(jnp.float32), start_of)
        length_of = jnp.where(match, user_length[u].astype(jnp.float32), length_of)
    half_of = (length_of - 1.0) * 0.5
    mid_of = start_of + half_of
    for c in range(chunks):
        mids[c * R : (c + 1) * R, :] = jnp.broadcast_to(mid_of[c : c + 1, :], (R, R)).T
        halves[c * R : (c + 1) * R, :] = jnp.broadcast_to(half_of[c : c + 1, :], (R, R)).T

    def project(c, weights):
        sums = [jnp.zeros((R, local), jnp.float32)] * 2
        for o in range(4):
            x = pieces[o, rows(c)]
            for i in range(2):
                sums[i] = sums[i] + jnp.dot(
                    x, weights[i, o * width : (o + 1) * width, :], preferred_element_type=jnp.float32
                )
        half = sums[1] * 0.5
        return sums[0].astype(jnp.bfloat16), half + half * jnp.tanh(half)

    def weigh(c, count, hop):
        here = pl.ds(pl.multiple_of(c * R, R), count * R)
        query = qg[0, here]
        repeat = BLOCK // R
        mid = jnp.concatenate([mids[here]] * repeat, axis=1)
        half_width = jnp.concatenate([halves[here]] * repeat, axis=1)
        lanes = lax.broadcasted_iota(jnp.int32, (1, BLOCK), 1)
        sums = [att[here, h * HDIM : (h + 1) * HDIM] for h in range(heads)]
        for b in range(hist_rows // BLOCK):
            places = (lanes + (hop * hist_rows + b * BLOCK)).astype(jnp.float32)
            inside = jnp.abs(places - mid) <= half_width
            for h in range(heads):
                cols = slice(h * HDIM, (h + 1) * HDIM)
                keys = kv[hop, 0, b * BLOCK : (b + 1) * BLOCK, cols]
                values = kv[hop, 1, b * BLOCK : (b + 1) * BLOCK, cols]
                score = lax.dot_general(
                    query[:, cols], keys, (((1,), (1,)), ((), ())), preferred_element_type=jnp.float32
                )
                x = score * (0.5 * HDIM**-0.5)
                weight = jnp.where(inside, x + x * jnp.tanh(x), 0.0).astype(jnp.bfloat16)
                sums[h] = sums[h] + jnp.dot(weight, values, preferred_element_type=jnp.float32)
        for h in range(heads):
            att[here, h * HDIM : (h + 1) * HDIM] = sums[h]

    def send_stats(c):
        attended = att[rows(c)]
        first = jnp.sum(attended, axis=1, keepdims=True)
        second = jnp.sum(attended * attended, axis=1, keepdims=True)
        lane = lax.broadcasted_iota(jnp.int32, (R, R), 1)
        both = jnp.where(lane == 0, first, jnp.where(lane == 1, second, 0.0))
        stats[t, c] = both.T[:8]
        for k in (1, 2, 3):
            stat_copy(c, k).start()

    def weigh_pair(p, hop):
        weigh(2 * p, 2, hop)

        @pl.when(hop == SPAN)
        def _():
            send_stats(2 * p)
            send_stats(2 * p + 1)

    def weigh_last(c):
        def step(hop, _):
            weigh(c, 1, hop)
            return 0

        lax.fori_loop(0, SPAN + 1, step, 0)
        send_stats(c)

    def finish(c, _):
        total = stats[t, c]
        for k in (1, 2, 3):
            stat_arrival(c, k).wait_recv()
            total = total + stats[lax.rem(t + k, 4), c]
        columns = jnp.concatenate([total, jnp.zeros((R - 8, R), jnp.float32)], axis=0).T
        mean = columns[:, 0:1] * (1.0 / HQ)
        var = columns[:, 1:2] * (1.0 / HQ) - mean * mean
        normed = (att[rows(c)] - mean) * lax.rsqrt(var + 1e-05)
        out[rows(c)] = (normed * gain[...] * gate[rows(c)]).astype(jnp.bfloat16)
        return 0

    early = chunks // 2
    paired = chunks - 2

    @pl.when(outer)
    def _():
        piece(1, t, in_of, 0).start()

        def send_step(c, _):
            piece(c - AHEAD, t, in_of, 0).wait_send()
            piece(c, t, in_of, 0).start()
            return 0

        lax.fori_loop(AHEAD, chunks // 2, send_step, 0)
        for which in range(2):
            kv_copy(0, which).wait_recv()
            kv_copy(1, which).start()
        lax.fori_loop(chunks // 2, chunks, send_step, 0)
        for c in range(chunks - AHEAD, chunks):
            piece(c, t, in_of, 0).wait_send()
        w_copy(w_own, place, 0, (s, in_of)).wait_send()
        for which in range(2):
            kv_copy(1, which).wait_recv()

        def take(c):
            for which in range(2):
                qg_copy(c, which, in_of).wait_recv()
            gate[rows(c)] = qg[1, rows(c)].astype(jnp.float32)

        def outer_pair(i, _):
            p, hop = i // (SPAN + 1), i % (SPAN + 1)

            @pl.when(hop == 0)
            def _():
                take(2 * p)
                take(2 * p + 1)

            weigh_pair(p, hop)
            return 0

        def outer_last(c, _):
            @pl.when(c == chunks - 1)
            def _():
                lax.fori_loop(0, early, finish, 0)

            take(c)
            weigh_last(c)
            return 0

        lax.fori_loop(0, paired // 2 * (SPAN + 1), outer_pair, 0)
        lax.fori_loop(paired, chunks, outer_last, 0)

    @pl.when(inner)
    def _():
        for c in range(AHEAD):
            piece(c, out_of, across, 1).wait_recv()
            piece(c, out_of, across, 1).start()
        w_copy(w_outer, place, 0, (s, t)).wait_recv()
        for k in (1, 2, 3):
            w_copy(w_outer, place, k, (base + peer_place(k), t)).start()
        w_copy(w_outer, place, 4, (sibling, t)).start()

        def project_outer(c, _):
            query, gated = project(c, w_outer)
            qg_outer[0, rows(c)] = query
            qg_outer[1, rows(c)] = gated.astype(jnp.bfloat16)
            for which in range(2):
                qg_copy(c, which, out_of).start()
            return 0

        def inner_item(i, _):
            p = jnp.where(i >= 6, 2, jnp.where((i == 2) | (i == 3) | (i == 5), 1, 0))
            hop = jnp.where(i >= 6, i - 6, jnp.where(i >= 4, 2, i % 2))
            weigh_pair(p, hop)
            return 0

        def bound(c):
            last = jnp.where(c == 4, 4, jnp.where(c == 5, 6, 9))
            return jnp.where(c <= 1, 0, jnp.where(c <= 3, c - 1, last))

        def inner_step(c, _):
            @pl.when(c + AHEAD < chunks)
            def _():
                piece(c + AHEAD, t, across, 0).start()
                piece(c + AHEAD, out_of, across, 1).wait_recv()
                piece(c + AHEAD, out_of, across, 1).start()

            @pl.when(c == 1)
            def _():
                for which in range(2):
                    kv_copy(0, which).wait_recv()
                    kv_copy(1, which).start()
                for k in (1, 2, 3):
                    w_copy(w_outer, peer_place(k), k, (sibling, t)).wait_recv()
                    w_copy(w_outer, peer_place(k), 4 + k, (sibling, t)).start()

            @pl.when(c == LAG)
            def _():
                for k in range(GROUP // 2):
                    w_copy(w_outer, peer_place(k) + 1 - 2 * core, 4 + k, (sibling, t)).wait_recv()

            @pl.when(c == LAG + 2)
            def _():
                for which in range(2):
                    kv_copy(1, which).wait_recv()

            @pl.when(c == chunks - 1)
            def _():
                lax.fori_loop(0, early, finish, 0)

            piece(c, across, across, 0).wait_recv()
            piece(c, 3 - out_of, across, 0).wait_recv()
            lax.fori_loop(jnp.where(c <= LAG, 0, c), jnp.where(c < LAG, 0, c + 1), project_outer, 0)
            query, gated = project(c, w_own)
            qg[0, rows(c)] = query
            gate[rows(c)] = gated
            lax.fori_loop(bound(c), bound(c + 1), inner_item, 0)

            @pl.when(c >= paired)
            def _():
                weigh_last(c)

            return 0

        lax.fori_loop(0, chunks, inner_step, 0)

    lax.fori_loop(early, chunks, finish, 0)

    for hop in range(SPAN):
        for which in range(2):
            kv_copy(hop, which).wait_send()

    def close_stats(c, _):
        for k in (1, 2, 3):
            stat_copy(c, k).wait_send()
        return 0

    lax.fori_loop(0, chunks, close_stats, 0)

    @pl.when(inner)
    def _():
        def close(c, _):
            piece(c, t, across, 0).wait_send()
            piece(c, out_of, across, 1).wait_send()
            for which in range(2):
                qg_copy(c, which, out_of).wait_send()
            return 0

        lax.fori_loop(0, chunks, close, 0)
        for k in (1, 2, 3):
            w_copy(w_outer, place, k, (base + peer_place(k), t)).wait_send()
        for k in range(GROUP // 2):
            w_copy(w_outer, peer_place(k), 4 + k, (sibling, t)).wait_send()


def body(
    n_seq, targets, w_query, w_gate, norm_gain, hist_keys, hist_values, user_offset, user_length, target_user
):
    rows_total, width = targets.shape
    depth, local = w_query.shape
    hist_rows = hist_keys.shape[0]
    chunks = rows_total // R
    anywhere = pl.BlockSpec(memory_space=pl.ANY)
    vmem = pl.BlockSpec(memory_space=pltpu.VMEM)
    smem = pl.BlockSpec(memory_space=pltpu.SMEM)
    dma = pltpu.SemaphoreType.DMA
    bf16, f32 = jnp.bfloat16, jnp.float32
    flops = 4 * rows_total * (1.5 * depth * local + (SPAN + 1) * hist_rows * local)
    return pl.pallas_call(
        functools.partial(kernel, n_seq),
        out_shape=jax.ShapeDtypeStruct((rows_total, local), bf16),
        in_specs=[anywhere, anywhere, anywhere, vmem, anywhere, anywhere, smem, smem, vmem],
        out_specs=vmem,
        scratch_shapes=[
            pltpu.VMEM((4, rows_total, width), bf16),
            pltpu.VMEM((2, depth, local), bf16),
            pltpu.VMEM((2, depth, local), bf16),
            pltpu.VMEM((SPAN + 1, 2, hist_rows, local), bf16),
            pltpu.VMEM((2, rows_total, local), bf16),
            pltpu.VMEM((2, rows_total, local), bf16),
            pltpu.VMEM((rows_total, local), f32),
            pltpu.VMEM((rows_total, local), f32),
            pltpu.VMEM((rows_total, R), f32),
            pltpu.VMEM((rows_total, R), f32),
            pltpu.VMEM((4, chunks, 8, R), f32),
            dma((5,)),
            dma((chunks, 2)),
            dma((chunks, 4)),
            dma((8,)),
            dma((GROUP,)),
            dma((SPAN, 2)),
            dma((SPAN, 2)),
            dma((chunks, 2)),
            dma((chunks, 2)),
            dma((chunks, 4)),
            dma((chunks, 4)),
        ],
        compiler_params=pltpu.CompilerParams(
            collective_id=0, has_side_effects=True, vmem_limit_bytes=60 * 1024 * 1024
        ),
        cost_estimate=pl.CostEstimate(flops=int(flops), bytes_accessed=5 * 1024 * 1024, transcendentals=0),
    )(
        targets,
        w_query,
        w_gate,
        norm_gain.reshape(1, local),
        hist_keys,
        hist_values,
        user_offset,
        user_length,
        target_user.reshape(chunks, R),
    )


def solution(mesh):
    return jax.shard_map(
        functools.partial(body, mesh.shape["seq"]),
        mesh=mesh,
        in_specs=(
            P("seq", "tp"),
            P(None, "tp"),
            P(None, "tp"),
            P("tp"),
            P("seq", "tp"),
            P("seq", "tp"),
            P("seq"),
            P("seq"),
            P("seq"),
        ),
        out_specs=P("seq", "tp"),
        check_vma=False,
    )
```

```python
import functools

import jax
import jax.numpy as jnp
from jax import lax
from jax.experimental import pallas as pl
from jax.experimental.pallas import tpu as pltpu
from jax.sharding import PartitionSpec as P

HDIM = 128
SPAN = 2
HQ = 1024
R = 128
BLOCK = 256
AHEAD = 2
DIRECT = 3
LAG = 3
FIRST = 4
GROUP = 8
MESH = pl.DeviceIdType.MESH


def kernel(
    n_seq,
    targets,
    w_query,
    w_gate,
    gain,
    hist_keys,
    hist_values,
    user_offset,
    user_length,
    target_user,
    out,
    pieces,
    w_own,
    w_outer,
    kv,
    qg,
    qg_outer,
    gate,
    att,
    mids,
    halves,
    stats,
    load_sem,
    piece_send,
    piece_recv,
    w_send,
    w_recv,
    kv_send,
    kv_recv,
    qg_send,
    qg_recv,
    stat_send,
    stat_recv,
):
    rows_total, width = targets.shape
    local = w_query.shape[1]
    heads = local // HDIM
    hist_rows = hist_keys.shape[0]
    users = user_offset.shape[0]
    chunks = rows_total // R
    s = lax.axis_index("seq")
    t = lax.axis_index("tp")
    inner = (t == 1) | (t == 2)
    outer = (t == 0) | (t == 3)
    out_of = 3 * (t - 1)
    across = 3 - t
    in_of = 1 + t // 3
    behind = lax.rem(s + n_seq - 1, n_seq)
    ahead = lax.rem(s + 1, n_seq)
    place = lax.rem(s, GROUP)
    base = s - place
    pair = place // 2
    core = lax.rem(place, 2)
    sibling = base + place + 1 - 2 * core
    w_rows = w_query.shape[0] // GROUP

    def rows(c):
        return pl.ds(pl.multiple_of(c * R, R), R)

    def remote(src, dst, send, recv, device):
        return pltpu.make_async_remote_copy(
            src_ref=src, dst_ref=dst, send_sem=send, recv_sem=recv, device_id=device, device_id_type=MESH
        )

    def piece(c, origin, to, which):
        ref = pieces.at[origin, rows(c)]
        return remote(ref, ref, piece_send.at[c, which], piece_recv.at[c, origin], (s, to))

    def w_slice(buffer, j):
        return buffer.at[:, pl.ds(pl.multiple_of(j * w_rows, w_rows), w_rows)]

    def w_copy(src, j, which, device):
        return remote(w_slice(src, j), w_slice(w_outer, j), w_send.at[which], w_recv.at[j], device)

    def peer_place(k):
        return lax.rem(pair + k, GROUP // 2) * 2 + core

    def kv_copy(hop, which):
        return remote(
            kv.at[hop, which], kv.at[hop + 1, which], kv_send.at[hop, which], kv_recv.at[hop, which], (behind, t)
        )

    def qg_copy(c, which, to):
        return remote(
            qg_outer.at[which, rows(c)], qg.at[which, rows(c)], qg_send.at[c, which], qg_recv.at[c, which], (s, to)
        )

    def stat_copy(c, k):
        peer = lax.rem(t + k, 4)
        return remote(stats.at[t, c], stats.at[t, c], stat_send.at[c, k], stat_recv.at[c, t], (s, peer))

    def stat_arrival(c, k):
        peer = lax.rem(t + k, 4)
        return remote(stats.at[peer, c], stats.at[peer, c], stat_send.at[c, k], stat_recv.at[c, peer], (s, peer))

    loads = [
        pltpu.make_async_copy(src, dst, load_sem.at[i])
        for i, (src, dst) in enumerate(
            [
                (targets, pieces.at[t]),
                (hist_keys, kv.at[0, 0]),
                (hist_values, kv.at[0, 1]),
                (w_query, w_own.at[0]),
                (w_gate, w_own.at[1]),
            ]
        )
    ]
    for load in loads:
        load.start()

    barrier = pltpu.get_barrier_semaphore()
    partners = [(s, lax.rem(t + k, 4)) for k in (1, 2, 3)]
    partners += [(behind, t), (ahead, t)]
    partners += [(base + peer_place(k), t) for k in (1, 2, 3)]
    partners += [(sibling, t)]
    for device in partners:
        pl.semaphore_signal(barrier, inc=1, device_id=device, device_id_type=MESH)
    pl.semaphore_wait(barrier, len(partners))

    loads[0].wait()

    @pl.when(outer)
    def _():
        for c in range(FIRST):
            piece(c, t, in_of, 0).start()

    @pl.when(inner)
    def _():
        for c in range(AHEAD):
            piece(c, t, across, 0).start()
        for c in range(DIRECT):
            piece(c, t, out_of, 2).start()

    for which in range(2):
        loads[1 + which].wait()
        kv_copy(0, which).start()
    for which in range(2):
        loads[3 + which].wait()

    @pl.when(outer)
    def _():
        w_copy(w_own, place, 0, (s, in_of)).start()

    att[...] = jnp.zeros(att.shape, jnp.float32)

    mine = target_user[...] - s * users
    start_of = jnp.zeros(mine.shape, jnp.float32)
    length_of = jnp.zeros(mine.shape, jnp.float32)
    for u in range(users):
        match = mine == u
        start_of = jnp.where(match, (user_offset[u] - s * hist_rows).astype(jnp.float32), start_of)
        length_of = jnp.where(match, user_length[u].astype(jnp.float32), length_of)
    half_of = (length_of - 1.0) * 0.5
    mid_of = start_of + half_of
    for c in range(chunks):
        mids[c * R : (c + 1) * R, :] = jnp.broadcast_to(mid_of[c : c + 1, :], (R, R)).T
        halves[c * R : (c + 1) * R, :] = jnp.broadcast_to(half_of[c : c + 1, :], (R, R)).T

    def project(c, weights):
        sums = [jnp.zeros((R, local), jnp.float32)] * 2
        for o in range(4):
            x = pieces[o, rows(c)]
            for i in range(2):
                sums[i] = sums[i] + jnp.dot(
                    x, weights[i, o * width : (o + 1) * width, :], preferred_element_type=jnp.float32
                )
        half = sums[1] * 0.5
        return sums[0].astype(jnp.bfloat16), half + half * jnp.tanh(half)

    def weigh(c, count, hop):
        here = pl.ds(pl.multiple_of(c * R, R), count * R)
        query = qg[0, here]
        repeat = BLOCK // R
        mid = jnp.concatenate([mids[here]] * repeat, axis=1)
        half_width = jnp.concatenate([halves[here]] * repeat, axis=1)
        lanes = lax.broadcasted_iota(jnp.int32, (1, BLOCK), 1)
        sums = [att[here, h * HDIM : (h + 1) * HDIM] for h in range(heads)]
        for b in range(hist_rows // BLOCK):
            places = (lanes + (hop * hist_rows + b * BLOCK)).astype(jnp.float32)
            inside = jnp.abs(places - mid) <= half_width
            for h in range(heads):
                cols = slice(h * HDIM, (h + 1) * HDIM)
                keys = kv[hop, 0, b * BLOCK : (b + 1) * BLOCK, cols]
                values = kv[hop, 1, b * BLOCK : (b + 1) * BLOCK, cols]
                score = lax.dot_general(
                    query[:, cols], keys, (((1,), (1,)), ((), ())), preferred_element_type=jnp.float32
                )
                x = score * (0.5 * HDIM**-0.5)
                weight = jnp.where(inside, x + x * jnp.tanh(x), 0.0).astype(jnp.bfloat16)
                sums[h] = sums[h] + jnp.dot(weight, values, preferred_element_type=jnp.float32)
        for h in range(heads):
            att[here, h * HDIM : (h + 1) * HDIM] = sums[h]

    def send_stats(c):
        attended = att[rows(c)]
        first = jnp.sum(attended, axis=1, keepdims=True)
        second = jnp.sum(attended * attended, axis=1, keepdims=True)
        lane = lax.broadcasted_iota(jnp.int32, (R, R), 1)
        both = jnp.where(lane == 0, first, jnp.where(lane == 1, second, 0.0))
        stats[t, c] = both.T[:8]
        for k in (1, 2, 3):
            stat_copy(c, k).start()

    def weigh_pair(p, hop):
        weigh(2 * p, 2, hop)

        @pl.when(hop == SPAN)
        def _():
            send_stats(2 * p)
            send_stats(2 * p + 1)

    def weigh_last(c):
        def step(hop, _):
            weigh(c, 1, hop)
            return 0

        lax.fori_loop(0, SPAN + 1, step, 0)
        send_stats(c)

    def finish(c, _):
        total = stats[t, c]
        for k in (1, 2, 3):
            stat_arrival(c, k).wait_recv()
            total = total + stats[lax.rem(t + k, 4), c]
        columns = jnp.concatenate([total, jnp.zeros((R - 8, R), jnp.float32)], axis=0).T
        mean = columns[:, 0:1] * (1.0 / HQ)
        var = columns[:, 1:2] * (1.0 / HQ) - mean * mean
        normed = (att[rows(c)] - mean) * lax.rsqrt(var + 1e-05)
        out[rows(c)] = (normed * gain[...] * gate[rows(c)]).astype(jnp.bfloat16)
        return 0

    early = chunks // 2
    paired = chunks - 2

    def take(c):
        for which in range(2):
            qg_copy(c, which, in_of).wait_recv()
        gate[rows(c)] = qg[1, rows(c)].astype(jnp.float32)

    def project_own(c):
        query, gated = project(c, w_own)
        qg[0, rows(c)] = query
        gate[rows(c)] = gated

    def project_outer(c, _):
        query, gated = project(c, w_outer)
        qg_outer[0, rows(c)] = query
        qg_outer[1, rows(c)] = gated.astype(jnp.bfloat16)
        for which in range(2):
            qg_copy(c, which, out_of).start()
        return 0

    @pl.when(inner)
    def _():
        for c in range(AHEAD):
            piece(c, out_of, across, 1).wait_recv()
            piece(c, out_of, across, 1).start()
        w_copy(w_outer, place, 0, (s, t)).wait_recv()
        for k in (1, 2, 3):
            w_copy(w_outer, place, k, (base + peer_place(k), t)).start()
        w_copy(w_outer, place, 4, (sibling, t)).start()

    def item(i, _):
        p = jnp.where(i >= 6, 2, jnp.where((i == 2) | (i == 3) | (i == 5), 1, 0))
        hop = jnp.where(i >= 6, i - 6, jnp.where(i >= 4, 2, i % 2))
        weigh_pair(p, hop)
        return 0

    def bound(c):
        last = jnp.where(c == 4, 4, jnp.where(c == 5, 6, 9))
        return jnp.where(c <= 1, 0, jnp.where(c <= 3, c - 1, last))

    def step(c, _):
        @pl.when(inner & (c + AHEAD < chunks))
        def _():
            piece(c + AHEAD, t, across, 0).start()
            piece(c + AHEAD, out_of, across, 1).wait_recv()
            piece(c + AHEAD, out_of, across, 1).start()

        @pl.when(outer & (c < (chunks - FIRST) // 2))
        def _():
            for i in range(2):
                piece(FIRST + 2 * c + i, t, in_of, 0).start()

        @pl.when(c == 1)
        def _():
            for which in range(2):
                kv_copy(0, which).wait_recv()
                kv_copy(1, which).start()

        @pl.when(inner & (c == LAG - 1))
        def _():
            for k in (1, 2, 3):
                w_copy(w_outer, peer_place(k), k, (sibling, t)).wait_recv()
                w_copy(w_outer, peer_place(k), 4 + k, (sibling, t)).start()

        @pl.when(c == 4)
        def _():
            for which in range(2):
                kv_copy(1, which).wait_recv()

        @pl.when(c == chunks - 1)
        def _():
            lax.fori_loop(0, early, finish, 0)

        @pl.when(inner)
        def _():
            piece(c, across, across, 0).wait_recv()
            piece(c, 3 - out_of, across, 0).wait_recv()

            @pl.when(c < DIRECT)
            def _():
                piece(c, across, out_of, 3).start()
                piece(c, 3 - out_of, out_of, 4).start()

            @pl.when(c == LAG)
            def _():
                for k in range(GROUP // 2):
                    w_copy(w_outer, peer_place(k) + 1 - 2 * core, 4 + k, (sibling, t)).wait_recv()

            lax.fori_loop(jnp.where(c <= LAG, DIRECT, c), jnp.where(c < LAG, DIRECT, c + 1), project_outer, 0)

        @pl.when(outer & (c < DIRECT))
        def _():
            for origin in (in_of, 3 - in_of, 3 - t):
                piece(c, origin, in_of, 0).wait_recv()

        @pl.when(inner | (c < DIRECT))
        def _():
            project_own(c)

        @pl.when(outer & (c >= DIRECT))
        def _():
            take(c)

        lax.fori_loop(bound(c), bound(c + 1), item, 0)

        @pl.when(c >= paired)
        def _():
            weigh_last(c)

        return 0

    lax.fori_loop(0, chunks, step, 0)
    lax.fori_loop(early, chunks, finish, 0)

    for hop in range(SPAN):
        for which in range(2):
            kv_copy(hop, which).wait_send()

    def close_stats(c, _):
        for k in (1, 2, 3):
            stat_copy(c, k).wait_send()
        return 0

    lax.fori_loop(0, chunks, close_stats, 0)

    @pl.when(outer)
    def _():
        def close(c, _):
            piece(c, t, in_of, 0).wait_send()
            return 0

        lax.fori_loop(0, chunks, close, 0)
        w_copy(w_own, place, 0, (s, in_of)).wait_send()

    @pl.when(inner)
    def _():
        def close(c, _):
            piece(c, t, across, 0).wait_send()
            piece(c, out_of, across, 1).wait_send()
            return 0

        def close_direct(c, _):
            piece(c, t, out_of, 2).wait_send()
            piece(c, across, out_of, 3).wait_send()
            piece(c, 3 - out_of, out_of, 4).wait_send()
            return 0

        def close_projected(c, _):
            for which in range(2):
                qg_copy(c, which, out_of).wait_send()
            return 0

        lax.fori_loop(0, chunks, close, 0)
        lax.fori_loop(0, DIRECT, close_direct, 0)
        lax.fori_loop(DIRECT, chunks, close_projected, 0)
        for k in (1, 2, 3):
            w_copy(w_outer, place, k, (base + peer_place(k), t)).wait_send()
        for k in range(GROUP // 2):
            w_copy(w_outer, peer_place(k), 4 + k, (sibling, t)).wait_send()


def body(
    n_seq, targets, w_query, w_gate, norm_gain, hist_keys, hist_values, user_offset, user_length, target_user
):
    rows_total, width = targets.shape
    depth, local = w_query.shape
    hist_rows = hist_keys.shape[0]
    chunks = rows_total // R
    anywhere = pl.BlockSpec(memory_space=pl.ANY)
    vmem = pl.BlockSpec(memory_space=pltpu.VMEM)
    smem = pl.BlockSpec(memory_space=pltpu.SMEM)
    dma = pltpu.SemaphoreType.DMA
    bf16, f32 = jnp.bfloat16, jnp.float32
    flops = 4 * rows_total * (1.5 * depth * local + (SPAN + 1) * hist_rows * local)
    return pl.pallas_call(
        functools.partial(kernel, n_seq),
        out_shape=jax.ShapeDtypeStruct((rows_total, local), bf16),
        in_specs=[anywhere, anywhere, anywhere, vmem, anywhere, anywhere, smem, smem, vmem],
        out_specs=vmem,
        scratch_shapes=[
            pltpu.VMEM((4, rows_total, width), bf16),
            pltpu.VMEM((2, depth, local), bf16),
            pltpu.VMEM((2, depth, local), bf16),
            pltpu.VMEM((SPAN + 1, 2, hist_rows, local), bf16),
            pltpu.VMEM((2, rows_total, local), bf16),
            pltpu.VMEM((2, rows_total, local), bf16),
            pltpu.VMEM((rows_total, local), f32),
            pltpu.VMEM((rows_total, local), f32),
            pltpu.VMEM((rows_total, R), f32),
            pltpu.VMEM((rows_total, R), f32),
            pltpu.VMEM((4, chunks, 8, R), f32),
            dma((5,)),
            dma((chunks, 5)),
            dma((chunks, 4)),
            dma((8,)),
            dma((GROUP,)),
            dma((SPAN, 2)),
            dma((SPAN, 2)),
            dma((chunks, 2)),
            dma((chunks, 2)),
            dma((chunks, 4)),
            dma((chunks, 4)),
        ],
        compiler_params=pltpu.CompilerParams(
            collective_id=0, has_side_effects=True, vmem_limit_bytes=60 * 1024 * 1024
        ),
        cost_estimate=pl.CostEstimate(flops=int(flops), bytes_accessed=5 * 1024 * 1024, transcendentals=0),
    )(
        targets,
        w_query,
        w_gate,
        norm_gain.reshape(1, local),
        hist_keys,
        hist_values,
        user_offset,
        user_length,
        target_user.reshape(chunks, R),
    )


def solution(mesh):
    return jax.shard_map(
        functools.partial(body, mesh.shape["seq"]),
        mesh=mesh,
        in_specs=(
            P("seq", "tp"),
            P(None, "tp"),
            P(None, "tp"),
            P("tp"),
            P("seq", "tp"),
            P("seq", "tp"),
            P("seq"),
            P("seq"),
            P("seq"),
        ),
        out_specs=P("seq", "tp"),
        check_vma=False,
    )
```

```python
import functools

import jax
import jax.numpy as jnp
from jax import lax
from jax.experimental import pallas as pl
from jax.experimental.pallas import tpu as pltpu
from jax.sharding import PartitionSpec as P

HDIM = 128
SPAN = 2
HQ = 1024
R = 128
BLOCK = 256
AHEAD = 4
DIRECT = 3
LAG = 3
FIRST = 4
GROUP = 8
MESH = pl.DeviceIdType.MESH


def kernel(
    n_seq,
    targets,
    w_query,
    w_gate,
    gain,
    hist_keys,
    hist_values,
    user_offset,
    user_length,
    target_user,
    out,
    pieces,
    w_own,
    w_outer,
    kv,
    qg,
    qg_outer,
    gate,
    att,
    mids,
    halves,
    stats,
    load_sem,
    piece_send,
    piece_recv,
    w_send,
    w_recv,
    kv_send,
    kv_recv,
    qg_send,
    qg_recv,
    stat_send,
    stat_recv,
):
    rows_total, width = targets.shape
    local = w_query.shape[1]
    heads = local // HDIM
    hist_rows = hist_keys.shape[0]
    users = user_offset.shape[0]
    chunks = rows_total // R
    s = lax.axis_index("seq")
    t = lax.axis_index("tp")
    inner = (t == 1) | (t == 2)
    outer = (t == 0) | (t == 3)
    out_of = 3 * (t - 1)
    across = 3 - t
    in_of = 1 + t // 3
    behind = lax.rem(s + n_seq - 1, n_seq)
    ahead = lax.rem(s + 1, n_seq)
    place = lax.rem(s, GROUP)
    base = s - place
    pair = place // 2
    core = lax.rem(place, 2)
    sibling = base + place + 1 - 2 * core
    w_rows = w_query.shape[0] // GROUP

    def rows(c):
        return pl.ds(pl.multiple_of(c * R, R), R)

    def remote(src, dst, send, recv, device):
        return pltpu.make_async_remote_copy(
            src_ref=src, dst_ref=dst, send_sem=send, recv_sem=recv, device_id=device, device_id_type=MESH
        )

    def piece(c, origin, to, which):
        ref = pieces.at[origin, rows(c)]
        return remote(ref, ref, piece_send.at[c, which], piece_recv.at[c, origin], (s, to))

    def w_slice(buffer, j):
        return buffer.at[:, pl.ds(pl.multiple_of(j * w_rows, w_rows), w_rows)]

    def w_copy(src, j, which, device):
        return remote(w_slice(src, j), w_slice(w_outer, j), w_send.at[which], w_recv.at[j], device)

    def peer_place(k):
        return lax.rem(pair + k, GROUP // 2) * 2 + core

    def kv_copy(hop, which):
        return remote(
            kv.at[hop, which], kv.at[hop + 1, which], kv_send.at[hop, which], kv_recv.at[hop, which], (behind, t)
        )

    def qg_copy(c, which, to):
        return remote(
            qg_outer.at[which, rows(c)], qg.at[which, rows(c)], qg_send.at[c, which], qg_recv.at[c, which], (s, to)
        )

    def stat_copy(c, k):
        peer = lax.rem(t + k, 4)
        return remote(stats.at[t, c], stats.at[t, c], stat_send.at[c, k], stat_recv.at[c, t], (s, peer))

    def stat_arrival(c, k):
        peer = lax.rem(t + k, 4)
        return remote(stats.at[peer, c], stats.at[peer, c], stat_send.at[c, k], stat_recv.at[c, peer], (s, peer))

    loads = [
        pltpu.make_async_copy(src, dst, load_sem.at[i])
        for i, (src, dst) in enumerate(
            [
                (targets, pieces.at[t]),
                (hist_keys, kv.at[0, 0]),
                (hist_values, kv.at[0, 1]),
                (w_query, w_own.at[0]),
                (w_gate, w_own.at[1]),
            ]
        )
    ]
    for load in loads:
        load.start()

    barrier = pltpu.get_barrier_semaphore()
    partners = [(s, lax.rem(t + k, 4)) for k in (1, 2, 3)]
    partners += [(behind, t), (ahead, t)]
    partners += [(base + peer_place(k), t) for k in (1, 2, 3)]
    partners += [(sibling, t)]
    for device in partners:
        pl.semaphore_signal(barrier, inc=1, device_id=device, device_id_type=MESH)
    pl.semaphore_wait(barrier, len(partners))

    loads[0].wait()

    @pl.when(outer)
    def _():
        for c in range(FIRST):
            piece(c, t, in_of, 0).start()

    @pl.when(inner)
    def _():
        for c in range(AHEAD):
            piece(c, t, across, 0).start()
        for c in range(DIRECT):
            piece(c, t, out_of, 2).start()

    for which in range(2):
        loads[1 + which].wait()
        kv_copy(0, which).start()
    for which in range(2):
        loads[3 + which].wait()

    @pl.when(outer)
    def _():
        w_copy(w_own, place, 0, (s, in_of)).start()

    att[...] = jnp.zeros(att.shape, jnp.float32)

    mine = target_user[...] - s * users
    start_of = jnp.zeros(mine.shape, jnp.float32)
    length_of = jnp.zeros(mine.shape, jnp.float32)
    for u in range(users):
        match = mine == u
        start_of = jnp.where(match, (user_offset[u] - s * hist_rows).astype(jnp.float32), start_of)
        length_of = jnp.where(match, user_length[u].astype(jnp.float32), length_of)
    half_of = (length_of - 1.0) * 0.5
    mid_of = start_of + half_of
    for c in range(chunks):
        mids[c * R : (c + 1) * R, :] = jnp.broadcast_to(mid_of[c : c + 1, :], (R, R)).T
        halves[c * R : (c + 1) * R, :] = jnp.broadcast_to(half_of[c : c + 1, :], (R, R)).T

    def project(c, weights):
        sums = [jnp.zeros((R, local), jnp.float32)] * 2
        for o in range(4):
            x = pieces[o, rows(c)]
            for i in range(2):
                sums[i] = sums[i] + jnp.dot(
                    x, weights[i, o * width : (o + 1) * width, :], preferred_element_type=jnp.float32
                )
        half = sums[1] * 0.5
        return sums[0].astype(jnp.bfloat16), half + half * jnp.tanh(half)

    def weigh(c, count, hop):
        here = pl.ds(pl.multiple_of(c * R, R), count * R)
        query = qg[0, here]
        repeat = BLOCK // R
        mid = jnp.concatenate([mids[here]] * repeat, axis=1)
        half_width = jnp.concatenate([halves[here]] * repeat, axis=1)
        lanes = lax.broadcasted_iota(jnp.int32, (1, BLOCK), 1)
        sums = [att[here, h * HDIM : (h + 1) * HDIM] for h in range(heads)]
        for b in range(hist_rows // BLOCK):
            places = (lanes + (hop * hist_rows + b * BLOCK)).astype(jnp.float32)
            inside = jnp.abs(places - mid) <= half_width
            for h in range(heads):
                cols = slice(h * HDIM, (h + 1) * HDIM)
                keys = kv[hop, 0, b * BLOCK : (b + 1) * BLOCK, cols]
                values = kv[hop, 1, b * BLOCK : (b + 1) * BLOCK, cols]
                score = lax.dot_general(
                    query[:, cols], keys, (((1,), (1,)), ((), ())), preferred_element_type=jnp.float32
                )
                x = score * (0.5 * HDIM**-0.5)
                weight = jnp.where(inside, x + x * jnp.tanh(x), 0.0).astype(jnp.bfloat16)
                sums[h] = sums[h] + jnp.dot(weight, values, preferred_element_type=jnp.float32)
        for h in range(heads):
            att[here, h * HDIM : (h + 1) * HDIM] = sums[h]

    def send_stats(c):
        attended = att[rows(c)]
        first = jnp.sum(attended, axis=1, keepdims=True)
        second = jnp.sum(attended * attended, axis=1, keepdims=True)
        lane = lax.broadcasted_iota(jnp.int32, (R, R), 1)
        both = jnp.where(lane == 0, first, jnp.where(lane == 1, second, 0.0))
        stats[t, c] = both.T[:8]
        for k in (1, 2, 3):
            stat_copy(c, k).start()

    def weigh_pair(p, hop):
        weigh(2 * p, 2, hop)

        @pl.when(hop == SPAN)
        def _():
            send_stats(2 * p)
            send_stats(2 * p + 1)

    def weigh_last(c):
        def step(hop, _):
            weigh(c, 1, hop)
            return 0

        lax.fori_loop(0, SPAN + 1, step, 0)
        send_stats(c)

    def finish(c, _):
        total = stats[t, c]
        for k in (1, 2, 3):
            stat_arrival(c, k).wait_recv()
            total = total + stats[lax.rem(t + k, 4), c]
        columns = jnp.concatenate([total, jnp.zeros((R - 8, R), jnp.float32)], axis=0).T
        mean = columns[:, 0:1] * (1.0 / HQ)
        var = columns[:, 1:2] * (1.0 / HQ) - mean * mean
        normed = (att[rows(c)] - mean) * lax.rsqrt(var + 1e-05)
        out[rows(c)] = (normed * gain[...] * gate[rows(c)]).astype(jnp.bfloat16)
        return 0

    early = chunks // 2
    paired = chunks - 2

    def take(c):
        for which in range(2):
            qg_copy(c, which, in_of).wait_recv()
        gate[rows(c)] = qg[1, rows(c)].astype(jnp.float32)

    def project_own(c):
        query, gated = project(c, w_own)
        qg[0, rows(c)] = query
        gate[rows(c)] = gated

    def project_outer(c, _):
        query, gated = project(c, w_outer)
        qg_outer[0, rows(c)] = query
        qg_outer[1, rows(c)] = gated.astype(jnp.bfloat16)
        for which in range(2):
            qg_copy(c, which, out_of).start()
        return 0

    @pl.when(inner)
    def _():
        for c in range(AHEAD):
            piece(c, out_of, across, 1).wait_recv()
            piece(c, out_of, across, 1).start()
        w_copy(w_outer, place, 0, (s, t)).wait_recv()
        for k in (1, 2, 3):
            w_copy(w_outer, place, k, (base + peer_place(k), t)).start()
        w_copy(w_outer, place, 4, (sibling, t)).start()

    def item(i, _):
        p = jnp.where(i >= 6, 2, jnp.where((i == 2) | (i == 3) | (i == 5), 1, 0))
        hop = jnp.where(i >= 6, i - 6, jnp.where(i >= 4, 2, i % 2))
        weigh_pair(p, hop)
        return 0

    def bound(c):
        last = jnp.where(c == 4, 4, jnp.where(c == 5, 6, 9))
        return jnp.where(c <= 1, 0, jnp.where(c <= 3, c - 1, last))

    def step(c, _):
        @pl.when(inner & (c + AHEAD < chunks))
        def _():
            piece(c + AHEAD, t, across, 0).start()
            piece(c + AHEAD, out_of, across, 1).wait_recv()
            piece(c + AHEAD, out_of, across, 1).start()

        @pl.when(outer & (c < (chunks - FIRST) // 2))
        def _():
            for i in range(2):
                piece(FIRST + 2 * c + i, t, in_of, 0).start()

        @pl.when(c == 1)
        def _():
            for which in range(2):
                kv_copy(0, which).wait_recv()
                kv_copy(1, which).start()

        @pl.when(inner & (c == LAG - 1))
        def _():
            for k in (1, 2, 3):
                w_copy(w_outer, peer_place(k), k, (sibling, t)).wait_recv()
                w_copy(w_outer, peer_place(k), 4 + k, (sibling, t)).start()

        @pl.when(c == 4)
        def _():
            for which in range(2):
                kv_copy(1, which).wait_recv()

        @pl.when(c == chunks - 1)
        def _():
            lax.fori_loop(0, early, finish, 0)

        @pl.when(inner)
        def _():
            piece(c, across, across, 0).wait_recv()
            piece(c, 3 - out_of, across, 0).wait_recv()

            @pl.when(c < DIRECT)
            def _():
                piece(c, across, out_of, 3).start()
                piece(c, 3 - out_of, out_of, 4).start()

            @pl.when(c == LAG)
            def _():
                for k in range(GROUP // 2):
                    w_copy(w_outer, peer_place(k) + 1 - 2 * core, 4 + k, (sibling, t)).wait_recv()

            lax.fori_loop(jnp.where(c <= LAG, DIRECT, c), jnp.where(c < LAG, DIRECT, c + 1), project_outer, 0)

        @pl.when(outer & (c < DIRECT))
        def _():
            for origin in (in_of, 3 - in_of, 3 - t):
                piece(c, origin, in_of, 0).wait_recv()

        @pl.when(inner | (c < DIRECT))
        def _():
            project_own(c)

        @pl.when(outer & (c >= DIRECT))
        def _():
            take(c)

        lax.fori_loop(bound(c), bound(c + 1), item, 0)

        @pl.when(c >= paired)
        def _():
            weigh_last(c)

        return 0

    lax.fori_loop(0, chunks, step, 0)
    lax.fori_loop(early, chunks, finish, 0)

    for hop in range(SPAN):
        for which in range(2):
            kv_copy(hop, which).wait_send()

    def close_stats(c, _):
        for k in (1, 2, 3):
            stat_copy(c, k).wait_send()
        return 0

    lax.fori_loop(0, chunks, close_stats, 0)

    @pl.when(outer)
    def _():
        def close(c, _):
            piece(c, t, in_of, 0).wait_send()
            return 0

        lax.fori_loop(0, chunks, close, 0)
        w_copy(w_own, place, 0, (s, in_of)).wait_send()

    @pl.when(inner)
    def _():
        def close(c, _):
            piece(c, t, across, 0).wait_send()
            piece(c, out_of, across, 1).wait_send()
            return 0

        def close_direct(c, _):
            piece(c, t, out_of, 2).wait_send()
            piece(c, across, out_of, 3).wait_send()
            piece(c, 3 - out_of, out_of, 4).wait_send()
            return 0

        def close_projected(c, _):
            for which in range(2):
                qg_copy(c, which, out_of).wait_send()
            return 0

        lax.fori_loop(0, chunks, close, 0)
        lax.fori_loop(0, DIRECT, close_direct, 0)
        lax.fori_loop(DIRECT, chunks, close_projected, 0)
        for k in (1, 2, 3):
            w_copy(w_outer, place, k, (base + peer_place(k), t)).wait_send()
        for k in range(GROUP // 2):
            w_copy(w_outer, peer_place(k), 4 + k, (sibling, t)).wait_send()


def body(
    n_seq, targets, w_query, w_gate, norm_gain, hist_keys, hist_values, user_offset, user_length, target_user
):
    rows_total, width = targets.shape
    depth, local = w_query.shape
    hist_rows = hist_keys.shape[0]
    chunks = rows_total // R
    anywhere = pl.BlockSpec(memory_space=pltpu.HBM)
    vmem = pl.BlockSpec(memory_space=pltpu.VMEM)
    smem = pl.BlockSpec(memory_space=pltpu.SMEM)
    dma = pltpu.SemaphoreType.DMA
    bf16, f32 = jnp.bfloat16, jnp.float32
    flops = 4 * rows_total * (1.5 * depth * local + (SPAN + 1) * hist_rows * local)
    return pl.pallas_call(
        functools.partial(kernel, n_seq),
        out_shape=jax.ShapeDtypeStruct((rows_total, local), bf16),
        in_specs=[anywhere, anywhere, anywhere, vmem, anywhere, anywhere, smem, smem, vmem],
        out_specs=vmem,
        scratch_shapes=[
            pltpu.VMEM((4, rows_total, width), bf16),
            pltpu.VMEM((2, depth, local), bf16),
            pltpu.VMEM((2, depth, local), bf16),
            pltpu.VMEM((SPAN + 1, 2, hist_rows, local), bf16),
            pltpu.VMEM((2, rows_total, local), bf16),
            pltpu.VMEM((2, rows_total, local), bf16),
            pltpu.VMEM((rows_total, local), f32),
            pltpu.VMEM((rows_total, local), f32),
            pltpu.VMEM((rows_total, R), f32),
            pltpu.VMEM((rows_total, R), f32),
            pltpu.VMEM((4, chunks, 8, R), f32),
            dma((5,)),
            dma((chunks, 5)),
            dma((chunks, 4)),
            dma((8,)),
            dma((GROUP,)),
            dma((SPAN, 2)),
            dma((SPAN, 2)),
            dma((chunks, 2)),
            dma((chunks, 2)),
            dma((chunks, 4)),
            dma((chunks, 4)),
        ],
        compiler_params=pltpu.CompilerParams(
            collective_id=0, has_side_effects=True, vmem_limit_bytes=40 * 1024 * 1024
        ),
        cost_estimate=pl.CostEstimate(flops=int(flops), bytes_accessed=5 * 1024 * 1024, transcendentals=0),
    )(
        targets,
        w_query,
        w_gate,
        norm_gain.reshape(1, local),
        hist_keys,
        hist_values,
        user_offset,
        user_length,
        target_user.reshape(chunks, R),
    )


def solution(mesh):
    return jax.shard_map(
        functools.partial(body, mesh.shape["seq"]),
        mesh=mesh,
        in_specs=(
            P("seq", "tp"),
            P(None, "tp"),
            P(None, "tp"),
            P("tp"),
            P("seq", "tp"),
            P("seq", "tp"),
            P("seq"),
            P("seq"),
            P("seq"),
        ),
        out_specs=P("seq", "tp"),
        check_vma=False,
    )
```

```python
import functools

import jax
import jax.numpy as jnp
from jax import lax
from jax.experimental import pallas as pl
from jax.experimental.pallas import tpu as pltpu
from jax.sharding import PartitionSpec as P

HDIM = 128
SPAN = 2
HQ = 1024
R = 128
BLOCK = 256
AHEAD = 4
PASSED = 3
DIRECT = 3
LAG = 3
FIRST = 4
GROUP = 8
MESH = pl.DeviceIdType.MESH


def kernel(
    n_seq,
    targets,
    w_query,
    w_gate,
    gain,
    hist_keys,
    hist_values,
    user_offset,
    user_length,
    target_user,
    out,
    pieces,
    w_own,
    w_outer,
    kv,
    qg,
    qg_outer,
    gate,
    att,
    mids,
    halves,
    stats,
    load_sem,
    piece_send,
    piece_recv,
    w_send,
    w_recv,
    kv_send,
    kv_recv,
    qg_send,
    qg_recv,
    stat_send,
    stat_recv,
):
    rows_total, width = targets.shape
    local = w_query.shape[1]
    heads = local // HDIM
    hist_rows = hist_keys.shape[0]
    users = user_offset.shape[0]
    chunks = rows_total // R
    s = lax.axis_index("seq")
    t = lax.axis_index("tp")
    inner = (t == 1) | (t == 2)
    outer = (t == 0) | (t == 3)
    out_of = 3 * (t - 1)
    across = 3 - t
    in_of = 1 + t // 3
    behind = lax.rem(s + n_seq - 1, n_seq)
    ahead = lax.rem(s + 1, n_seq)
    place = lax.rem(s, GROUP)
    base = s - place
    core = lax.rem(place, 2)
    sibling = base + place + 1 - 2 * core
    w_rows = w_query.shape[0] // GROUP

    def rows(c):
        return pl.ds(pl.multiple_of(c * R, R), R)

    def remote(src, dst, send, recv, device):
        return pltpu.make_async_remote_copy(
            src_ref=src, dst_ref=dst, send_sem=send, recv_sem=recv, device_id=device, device_id_type=MESH
        )

    def piece(c, origin, to, which):
        ref = pieces.at[origin, rows(c)]
        return remote(ref, ref, piece_send.at[c, which], piece_recv.at[c, origin], (s, to))

    def w_slice(buffer, j):
        return buffer.at[:, pl.ds(pl.multiple_of(j * w_rows, w_rows), w_rows)]

    def w_copy(src, j, which, device):
        return remote(w_slice(src, j), w_slice(w_outer, j), w_send.at[which], w_recv.at[j], device)

    bit = lax.rem(place // 2, 2)
    beside = place + 2 - 4 * bit
    over = place + 4 - 8 * (place // 4)
    corner = over + 2 - 4 * bit
    quarter = (place, beside, over, corner)

    def kv_copy(hop, which):
        return remote(
            kv.at[hop, which], kv.at[hop + 1, which], kv_send.at[hop, which], kv_recv.at[hop, which], (behind, t)
        )

    def qg_copy(c, which, to):
        return remote(
            qg_outer.at[which, rows(c)], qg.at[which, rows(c)], qg_send.at[c, which], qg_recv.at[c, which], (s, to)
        )

    def stat_copy(c, k):
        peer = lax.rem(t + k, 4)
        return remote(stats.at[t, c], stats.at[t, c], stat_send.at[c, k], stat_recv.at[c, t], (s, peer))

    def stat_arrival(c, k):
        peer = lax.rem(t + k, 4)
        return remote(stats.at[peer, c], stats.at[peer, c], stat_send.at[c, k], stat_recv.at[c, peer], (s, peer))

    loads = [
        pltpu.make_async_copy(src, dst, load_sem.at[i])
        for i, (src, dst) in enumerate(
            [
                (targets, pieces.at[t]),
                (hist_keys, kv.at[0, 0]),
                (hist_values, kv.at[0, 1]),
                (w_query, w_own.at[0]),
                (w_gate, w_own.at[1]),
            ]
        )
    ]
    for load in loads:
        load.start()

    barrier = pltpu.get_barrier_semaphore()
    partners = [(s, lax.rem(t + k, 4)) for k in (1, 2, 3)]
    partners += [(behind, t), (ahead, t)]
    partners += [(base + beside, t), (base + over, t)]
    partners += [(sibling, t)]
    for device in partners:
        pl.semaphore_signal(barrier, inc=1, device_id=device, device_id_type=MESH)
    pl.semaphore_wait(barrier, len(partners))

    loads[3].wait()
    loads[4].wait()

    @pl.when(outer)
    def _():
        w_copy(w_own, place, 0, (s, in_of)).start()

    loads[0].wait()

    @pl.when(outer)
    def _():
        for c in range(FIRST):
            piece(c, t, in_of, 0).start()

    @pl.when(inner)
    def _():
        for c in range(AHEAD):
            piece(c, t, across, 0).start()
        for c in range(DIRECT):
            piece(c, t, out_of, 2).start()

    for which in range(2):
        loads[1 + which].wait()
        kv_copy(0, which).start()
    att[...] = jnp.zeros(att.shape, jnp.float32)

    mine = target_user[...] - s * users
    start_of = jnp.zeros(mine.shape, jnp.float32)
    length_of = jnp.zeros(mine.shape, jnp.float32)
    for u in range(users):
        match = mine == u
        start_of = jnp.where(match, (user_offset[u] - s * hist_rows).astype(jnp.float32), start_of)
        length_of = jnp.where(match, user_length[u].astype(jnp.float32), length_of)
    half_of = (length_of - 1.0) * 0.5
    mid_of = start_of + half_of
    for c in range(chunks):
        mids[c * R : (c + 1) * R, :] = jnp.broadcast_to(mid_of[c : c + 1, :], (R, R)).T
        halves[c * R : (c + 1) * R, :] = jnp.broadcast_to(half_of[c : c + 1, :], (R, R)).T

    def project(c, weights):
        sums = [jnp.zeros((R, local), jnp.float32)] * 2
        for o in range(4):
            x = pieces[o, rows(c)]
            for i in range(2):
                sums[i] = sums[i] + jnp.dot(
                    x, weights[i, o * width : (o + 1) * width, :], preferred_element_type=jnp.float32
                )
        half = sums[1] * 0.5
        return sums[0].astype(jnp.bfloat16), half + half * jnp.tanh(half)

    def weigh(c, count, hop):
        here = pl.ds(pl.multiple_of(c * R, R), count * R)
        query = qg[0, here]
        repeat = BLOCK // R
        mid = jnp.concatenate([mids[here]] * repeat, axis=1)
        half_width = jnp.concatenate([halves[here]] * repeat, axis=1)
        lanes = lax.broadcasted_iota(jnp.int32, (1, BLOCK), 1)
        sums = [att[here, h * HDIM : (h + 1) * HDIM] for h in range(heads)]
        for b in range(hist_rows // BLOCK):
            places = (lanes + (hop * hist_rows + b * BLOCK)).astype(jnp.float32)
            inside = jnp.abs(places - mid) <= half_width
            for h in range(heads):
                cols = slice(h * HDIM, (h + 1) * HDIM)
                keys = kv[hop, 0, b * BLOCK : (b + 1) * BLOCK, cols]
                values = kv[hop, 1, b * BLOCK : (b + 1) * BLOCK, cols]
                score = lax.dot_general(
                    query[:, cols], keys, (((1,), (1,)), ((), ())), preferred_element_type=jnp.float32
                )
                x = score * (0.5 * HDIM**-0.5)
                weight = jnp.where(inside, x + x * jnp.tanh(x), 0.0).astype(jnp.bfloat16)
                sums[h] = sums[h] + jnp.dot(weight, values, preferred_element_type=jnp.float32)
        for h in range(heads):
            att[here, h * HDIM : (h + 1) * HDIM] = sums[h]

    def send_stats(c):
        attended = att[rows(c)]
        first = jnp.sum(attended, axis=1, keepdims=True)
        second = jnp.sum(attended * attended, axis=1, keepdims=True)
        lane = lax.broadcasted_iota(jnp.int32, (R, R), 1)
        both = jnp.where(lane == 0, first, jnp.where(lane == 1, second, 0.0))
        stats[t, c] = both.T[:8]
        for k in (1, 2, 3):
            stat_copy(c, k).start()

    def weigh_pair(p, hop):
        weigh(2 * p, 2, hop)

        @pl.when(hop == SPAN)
        def _():
            send_stats(2 * p)
            send_stats(2 * p + 1)

    def weigh_last(c):
        def step(hop, _):
            weigh(c, 1, hop)
            return 0

        lax.fori_loop(0, SPAN + 1, step, 0)
        send_stats(c)

    def finish(c, _):
        total = stats[t, c]
        for k in (1, 2, 3):
            stat_arrival(c, k).wait_recv()
            total = total + stats[lax.rem(t + k, 4), c]
        columns = jnp.concatenate([total, jnp.zeros((R - 8, R), jnp.float32)], axis=0).T
        mean = columns[:, 0:1] * (1.0 / HQ)
        var = columns[:, 1:2] * (1.0 / HQ) - mean * mean
        normed = (att[rows(c)] - mean) * lax.rsqrt(var + 1e-05)
        out[rows(c)] = (normed * gain[...] * gate[rows(c)]).astype(jnp.bfloat16)
        return 0

    early = chunks // 2
    paired = chunks - 2

    def take(c):
        for which in range(2):
            qg_copy(c, which, in_of).wait_recv()
        gate[rows(c)] = qg[1, rows(c)].astype(jnp.float32)

    def project_own(c):
        query, gated = project(c, w_own)
        qg[0, rows(c)] = query
        gate[rows(c)] = gated

    def project_outer(c, _):
        query, gated = project(c, w_outer)
        qg_outer[0, rows(c)] = query
        qg_outer[1, rows(c)] = gated.astype(jnp.bfloat16)
        for which in range(2):
            qg_copy(c, which, out_of).start()
        return 0

    @pl.when(inner)
    def _():
        w_copy(w_outer, place, 0, (s, t)).wait_recv()
        w_copy(w_outer, place, 1, (base + beside, t)).start()
        w_copy(w_outer, place, 4, (sibling, t)).start()
        for c in range(PASSED):
            piece(c, out_of, across, 1).wait_recv()
            piece(c, out_of, across, 1).start()
        w_copy(w_outer, beside, 1, (base + beside, t)).wait_recv()
        w_copy(w_outer, place, 2, (base + over, t)).start()
        w_copy(w_outer, beside, 3, (base + over, t)).start()
        w_copy(w_outer, beside, 5, (sibling, t)).start()

    def item(i, _):
        p = jnp.where(i >= 6, 2, jnp.where((i == 2) | (i == 3) | (i == 5), 1, 0))
        hop = jnp.where(i >= 6, i - 6, jnp.where(i >= 4, 2, i % 2))
        weigh_pair(p, hop)
        return 0

    def bound(c):
        last = jnp.where(c == 4, 4, jnp.where(c == 5, 6, 9))
        return jnp.where(c <= 1, 0, jnp.where(c <= 3, c - 1, last))

    def step(c, _):
        @pl.when(inner & (c + AHEAD < chunks))
        def _():
            piece(c + AHEAD, t, across, 0).start()

        @pl.when(inner & (c + PASSED < chunks))
        def _():
            piece(c + PASSED, out_of, across, 1).wait_recv()
            piece(c + PASSED, out_of, across, 1).start()

        @pl.when(outer & (c < (chunks - FIRST) // 2))
        def _():
            for i in range(2):
                piece(FIRST + 2 * c + i, t, in_of, 0).start()

        @pl.when(c == 1)
        def _():
            for which in range(2):
                kv_copy(0, which).wait_recv()
                kv_copy(1, which).start()

        @pl.when(inner & (c == 1))
        def _():
            for k in (2, 3):
                w_copy(w_outer, quarter[k], k, (sibling, t)).wait_recv()
                w_copy(w_outer, quarter[k], 4 + k, (sibling, t)).start()

        @pl.when(c == 4)
        def _():
            for which in range(2):
                kv_copy(1, which).wait_recv()

        @pl.when(c == chunks - 1)
        def _():
            lax.fori_loop(0, early, finish, 0)

        @pl.when(inner)
        def _():
            piece(c, across, across, 0).wait_recv()
            piece(c, 3 - out_of, across, 0).wait_recv()

            @pl.when(c < DIRECT)
            def _():
                piece(c, across, out_of, 3).start()
                piece(c, 3 - out_of, out_of, 4).start()

            @pl.when(c == LAG)
            def _():
                for k in range(4):
                    w_copy(w_outer, quarter[k] + 1 - 2 * core, 4 + k, (sibling, t)).wait_recv()

            lax.fori_loop(jnp.where(c <= LAG, DIRECT, c), jnp.where(c < LAG, DIRECT, c + 1), project_outer, 0)

        @pl.when(outer & (c < DIRECT))
        def _():
            for origin in (in_of, 3 - in_of, 3 - t):
                piece(c, origin, in_of, 0).wait_recv()

        @pl.when(inner | (c < DIRECT))
        def _():
            project_own(c)

        @pl.when(outer & (c >= DIRECT))
        def _():
            take(c)

        lax.fori_loop(bound(c), bound(c + 1), item, 0)

        @pl.when(c >= paired)
        def _():
            weigh_last(c)

        return 0

    lax.fori_loop(0, chunks, step, 0)
    lax.fori_loop(early, chunks, finish, 0)

    for hop in range(SPAN):
        for which in range(2):
            kv_copy(hop, which).wait_send()

    def close_stats(c, _):
        for k in (1, 2, 3):
            stat_copy(c, k).wait_send()
        return 0

    lax.fori_loop(0, chunks, close_stats, 0)

    @pl.when(outer)
    def _():
        def close(c, _):
            piece(c, t, in_of, 0).wait_send()
            return 0

        lax.fori_loop(0, chunks, close, 0)
        w_copy(w_own, place, 0, (s, in_of)).wait_send()

    @pl.when(inner)
    def _():
        def close(c, _):
            piece(c, t, across, 0).wait_send()
            piece(c, out_of, across, 1).wait_send()
            return 0

        def close_direct(c, _):
            piece(c, t, out_of, 2).wait_send()
            piece(c, across, out_of, 3).wait_send()
            piece(c, 3 - out_of, out_of, 4).wait_send()
            return 0

        def close_projected(c, _):
            for which in range(2):
                qg_copy(c, which, out_of).wait_send()
            return 0

        lax.fori_loop(0, chunks, close, 0)
        lax.fori_loop(0, DIRECT, close_direct, 0)
        lax.fori_loop(DIRECT, chunks, close_projected, 0)
        w_copy(w_outer, place, 1, (base + beside, t)).wait_send()
        w_copy(w_outer, place, 2, (base + over, t)).wait_send()
        w_copy(w_outer, beside, 3, (base + over, t)).wait_send()
        for k in range(4):
            w_copy(w_outer, quarter[k], 4 + k, (sibling, t)).wait_send()


def body(
    n_seq, targets, w_query, w_gate, norm_gain, hist_keys, hist_values, user_offset, user_length, target_user
):
    rows_total, width = targets.shape
    depth, local = w_query.shape
    hist_rows = hist_keys.shape[0]
    chunks = rows_total // R
    anywhere = pl.BlockSpec(memory_space=pltpu.HBM)
    vmem = pl.BlockSpec(memory_space=pltpu.VMEM)
    smem = pl.BlockSpec(memory_space=pltpu.SMEM)
    dma = pltpu.SemaphoreType.DMA
    bf16, f32 = jnp.bfloat16, jnp.float32
    flops = 4 * rows_total * (1.5 * depth * local + (SPAN + 1) * hist_rows * local)
    return pl.pallas_call(
        functools.partial(kernel, n_seq),
        out_shape=jax.ShapeDtypeStruct((rows_total, local), bf16),
        in_specs=[anywhere, anywhere, anywhere, vmem, anywhere, anywhere, smem, smem, vmem],
        out_specs=vmem,
        scratch_shapes=[
            pltpu.VMEM((4, rows_total, width), bf16),
            pltpu.VMEM((2, depth, local), bf16),
            pltpu.VMEM((2, depth, local), bf16),
            pltpu.VMEM((SPAN + 1, 2, hist_rows, local), bf16),
            pltpu.VMEM((2, rows_total, local), bf16),
            pltpu.VMEM((2, rows_total, local), bf16),
            pltpu.VMEM((rows_total, local), f32),
            pltpu.VMEM((rows_total, local), f32),
            pltpu.VMEM((rows_total, R), f32),
            pltpu.VMEM((rows_total, R), f32),
            pltpu.VMEM((4, chunks, 8, R), f32),
            dma((5,)),
            dma((chunks, 5)),
            dma((chunks, 4)),
            dma((8,)),
            dma((GROUP,)),
            dma((SPAN, 2)),
            dma((SPAN, 2)),
            dma((chunks, 2)),
            dma((chunks, 2)),
            dma((chunks, 4)),
            dma((chunks, 4)),
        ],
        compiler_params=pltpu.CompilerParams(
            collective_id=0, has_side_effects=True, vmem_limit_bytes=60 * 1024 * 1024
        ),
        cost_estimate=pl.CostEstimate(flops=int(flops), bytes_accessed=5 * 1024 * 1024, transcendentals=0),
    )(
        targets,
        w_query,
        w_gate,
        norm_gain.reshape(1, local),
        hist_keys,
        hist_values,
        user_offset,
        user_length,
        target_user.reshape(chunks, R),
    )


def solution(mesh):
    return jax.shard_map(
        functools.partial(body, mesh.shape["seq"]),
        mesh=mesh,
        in_specs=(
            P("seq", "tp"),
            P(None, "tp"),
            P(None, "tp"),
            P("tp"),
            P("seq", "tp"),
            P("seq", "tp"),
            P("seq"),
            P("seq"),
            P("seq"),
        ),
        out_specs=P("seq", "tp"),
        check_vma=False,
    )
```

```python
import functools

import jax
import jax.numpy as jnp
from jax import lax
from jax.experimental import pallas as pl
from jax.experimental.pallas import tpu as pltpu
from jax.sharding import PartitionSpec as P

HDIM = 128
SPAN = 2
HQ = 1024
R = 128
BLOCK = 256
AHEAD = 4
PASSED = 3
DIRECT = 3
LAG = 3
FIRST = 4
GROUP = 8
MESH = pl.DeviceIdType.MESH


def kernel(
    n_seq,
    targets,
    w_query,
    w_gate,
    gain,
    hist_keys,
    hist_values,
    user_offset,
    user_length,
    target_user,
    out,
    pieces,
    w_own,
    w_outer,
    kv,
    qg,
    qg_outer,
    gate,
    att,
    mids,
    halves,
    stats,
    load_sem,
    piece_send,
    piece_recv,
    w_send,
    w_recv,
    kv_send,
    kv_recv,
    qg_send,
    qg_recv,
    stat_send,
    stat_recv,
):
    rows_total, width = targets.shape
    local = w_query.shape[1]
    heads = local // HDIM
    hist_rows = hist_keys.shape[0]
    users = user_offset.shape[0]
    chunks = rows_total // R
    s = lax.axis_index("seq")
    t = lax.axis_index("tp")
    inner = (t == 1) | (t == 2)
    outer = (t == 0) | (t == 3)
    out_of = 3 * (t - 1)
    across = 3 - t
    in_of = 1 + t // 3
    behind = lax.rem(s + n_seq - 1, n_seq)
    ahead = lax.rem(s + 1, n_seq)
    behind2 = lax.rem(s + n_seq - 2, n_seq)
    ahead2 = lax.rem(s + 2, n_seq)
    odd = lax.rem(s, 2) == 1
    place = lax.rem(s, GROUP)
    base = s - place
    core = lax.rem(place, 2)
    sibling = base + place + 1 - 2 * core
    w_rows = w_query.shape[0] // GROUP

    def rows(c):
        return pl.ds(pl.multiple_of(c * R, R), R)

    def remote(src, dst, send, recv, device):
        return pltpu.make_async_remote_copy(
            src_ref=src, dst_ref=dst, send_sem=send, recv_sem=recv, device_id=device, device_id_type=MESH
        )

    def piece(c, origin, to, which):
        ref = pieces.at[origin, rows(c)]
        return remote(ref, ref, piece_send.at[c, which], piece_recv.at[c, origin], (s, to))

    def w_slice(buffer, j):
        return buffer.at[:, pl.ds(pl.multiple_of(j * w_rows, w_rows), w_rows)]

    def w_copy(src, j, which, device):
        return remote(w_slice(src, j), w_slice(w_outer, j), w_send.at[which], w_recv.at[j], device)

    bit = lax.rem(place // 2, 2)
    beside = place + 2 - 4 * bit
    over = place + 4 - 8 * (place // 4)
    corner = over + 2 - 4 * bit
    quarter = (place, beside, over, corner)

    def kv_copy(hop, which):
        return remote(
            kv.at[hop, which], kv.at[hop + 1, which], kv_send.at[hop, which], kv_recv.at[hop, which], (behind, t)
        )

    def kv_skip(which):
        return remote(kv.at[0, which], kv.at[2, which], kv_send.at[2, which], kv_recv.at[1, which], (behind2, t))

    def qg_copy(c, which, to):
        return remote(
            qg_outer.at[which, rows(c)], qg.at[which, rows(c)], qg_send.at[c, which], qg_recv.at[c, which], (s, to)
        )

    def stat_copy(c, k):
        peer = lax.rem(t + k, 4)
        return remote(stats.at[t, c], stats.at[t, c], stat_send.at[c, k], stat_recv.at[c, t], (s, peer))

    def stat_arrival(c, k):
        peer = lax.rem(t + k, 4)
        return remote(stats.at[peer, c], stats.at[peer, c], stat_send.at[c, k], stat_recv.at[c, peer], (s, peer))

    loads = [
        pltpu.make_async_copy(src, dst, load_sem.at[i])
        for i, (src, dst) in enumerate(
            [
                (targets, pieces.at[t]),
                (hist_keys, kv.at[0, 0]),
                (hist_values, kv.at[0, 1]),
                (w_query, w_own.at[0]),
                (w_gate, w_own.at[1]),
            ]
        )
    ]
    for load in loads:
        load.start()

    barrier = pltpu.get_barrier_semaphore()
    partners = [(s, lax.rem(t + k, 4)) for k in (1, 2, 3)]
    partners += [(behind, t), (ahead, t), (behind2, t), (ahead2, t)]
    partners += [(base + beside, t), (base + over, t)]
    partners += [(sibling, t)]
    for device in partners:
        pl.semaphore_signal(barrier, inc=1, device_id=device, device_id_type=MESH)
    pl.semaphore_wait(barrier, len(partners))

    loads[3].wait()
    loads[4].wait()

    @pl.when(outer)
    def _():
        w_copy(w_own, place, 0, (s, in_of)).start()

    loads[0].wait()

    @pl.when(outer)
    def _():
        for c in range(FIRST):
            piece(c, t, in_of, 0).start()

    @pl.when(inner)
    def _():
        for c in range(AHEAD):
            piece(c, t, across, 0).start()
        for c in range(DIRECT):
            piece(c, t, out_of, 2).start()

    for which in range(2):
        loads[1 + which].wait()
        kv_copy(0, which).start()
    att[...] = jnp.zeros(att.shape, jnp.float32)

    mine = target_user[...] - s * users
    start_of = jnp.zeros(mine.shape, jnp.float32)
    length_of = jnp.zeros(mine.shape, jnp.float32)
    for u in range(users):
        match = mine == u
        start_of = jnp.where(match, (user_offset[u] - s * hist_rows).astype(jnp.float32), start_of)
        length_of = jnp.where(match, user_length[u].astype(jnp.float32), length_of)
    half_of = (length_of - 1.0) * 0.5
    mid_of = start_of + half_of
    for c in range(chunks):
        mids[c * R : (c + 1) * R, :] = jnp.broadcast_to(mid_of[c : c + 1, :], (R, R)).T
        halves[c * R : (c + 1) * R, :] = jnp.broadcast_to(half_of[c : c + 1, :], (R, R)).T

    def project(c, weights):
        sums = [jnp.zeros((R, local), jnp.float32)] * 2
        for o in range(4):
            x = pieces[o, rows(c)]
            for i in range(2):
                sums[i] = sums[i] + jnp.dot(
                    x, weights[i, o * width : (o + 1) * width, :], preferred_element_type=jnp.float32
                )
        half = sums[1] * 0.5
        return sums[0].astype(jnp.bfloat16), half + half * jnp.tanh(half)

    def weigh(c, count, hop):
        here = pl.ds(pl.multiple_of(c * R, R), count * R)
        query = qg[0, here]
        repeat = BLOCK // R
        mid = jnp.concatenate([mids[here]] * repeat, axis=1)
        half_width = jnp.concatenate([halves[here]] * repeat, axis=1)
        lanes = lax.broadcasted_iota(jnp.int32, (1, BLOCK), 1)
        sums = [att[here, h * HDIM : (h + 1) * HDIM] for h in range(heads)]
        for b in range(hist_rows // BLOCK):
            places = (lanes + (hop * hist_rows + b * BLOCK)).astype(jnp.float32)
            inside = jnp.abs(places - mid) <= half_width
            for h in range(heads):
                cols = slice(h * HDIM, (h + 1) * HDIM)
                keys = kv[hop, 0, b * BLOCK : (b + 1) * BLOCK, cols]
                values = kv[hop, 1, b * BLOCK : (b + 1) * BLOCK, cols]
                score = lax.dot_general(
                    query[:, cols], keys, (((1,), (1,)), ((), ())), preferred_element_type=jnp.float32
                )
                x = score * (0.5 * HDIM**-0.5)
                weight = jnp.where(inside, x + x * jnp.tanh(x), 0.0).astype(jnp.bfloat16)
                sums[h] = sums[h] + jnp.dot(weight, values, preferred_element_type=jnp.float32)
        for h in range(heads):
            att[here, h * HDIM : (h + 1) * HDIM] = sums[h]

    def send_stats(c):
        attended = att[rows(c)]
        first = jnp.sum(attended, axis=1, keepdims=True)
        second = jnp.sum(attended * attended, axis=1, keepdims=True)
        lane = lax.broadcasted_iota(jnp.int32, (R, R), 1)
        both = jnp.where(lane == 0, first, jnp.where(lane == 1, second, 0.0))
        stats[t, c] = both.T[:8]
        for k in (1, 2, 3):
            stat_copy(c, k).start()

    def weigh_pair(p, hop):
        weigh(2 * p, 2, hop)

        @pl.when(hop == SPAN)
        def _():
            send_stats(2 * p)
            send_stats(2 * p + 1)

    def weigh_last(c):
        def step(hop, _):
            weigh(c, 1, hop)
            return 0

        lax.fori_loop(0, SPAN + 1, step, 0)
        send_stats(c)

    def finish(c, _):
        total = stats[t, c]
        for k in (1, 2, 3):
            stat_arrival(c, k).wait_recv()
            total = total + stats[lax.rem(t + k, 4), c]
        columns = jnp.concatenate([total, jnp.zeros((R - 8, R), jnp.float32)], axis=0).T
        mean = columns[:, 0:1] * (1.0 / HQ)
        var = columns[:, 1:2] * (1.0 / HQ) - mean * mean
        normed = (att[rows(c)] - mean) * lax.rsqrt(var + 1e-05)
        out[rows(c)] = (normed * gain[...] * gate[rows(c)]).astype(jnp.bfloat16)
        return 0

    early = chunks // 2
    paired = chunks - 2

    def take(c):
        for which in range(2):
            qg_copy(c, which, in_of).wait_recv()
        gate[rows(c)] = qg[1, rows(c)].astype(jnp.float32)

    def project_own(c):
        query, gated = project(c, w_own)
        qg[0, rows(c)] = query
        gate[rows(c)] = gated

    def project_outer(c, _):
        query, gated = project(c, w_outer)
        qg_outer[0, rows(c)] = query
        qg_outer[1, rows(c)] = gated.astype(jnp.bfloat16)
        for which in range(2):
            qg_copy(c, which, out_of).start()
        return 0

    @pl.when(inner)
    def _():
        w_copy(w_outer, place, 0, (s, t)).wait_recv()
        w_copy(w_outer, place, 1, (base + beside, t)).start()
        w_copy(w_outer, place, 4, (sibling, t)).start()
        for c in range(PASSED):
            piece(c, out_of, across, 1).wait_recv()
            piece(c, out_of, across, 1).start()
        w_copy(w_outer, beside, 1, (base + beside, t)).wait_recv()
        w_copy(w_outer, place, 2, (base + over, t)).start()
        w_copy(w_outer, beside, 3, (base + over, t)).start()
        w_copy(w_outer, beside, 5, (sibling, t)).start()

    def item(i, _):
        p = jnp.where(i >= 6, 2, jnp.where((i == 2) | (i == 3) | (i == 5), 1, 0))
        hop = jnp.where(i >= 6, i - 6, jnp.where(i >= 4, 2, i % 2))
        weigh_pair(p, hop)
        return 0

    def bound(c):
        last = jnp.where(c == 4, 4, jnp.where(c == 5, 6, 9))
        return jnp.where(c <= 1, 0, jnp.where(c <= 3, c - 1, last))

    def step(c, _):
        @pl.when(inner & (c + AHEAD < chunks))
        def _():
            piece(c + AHEAD, t, across, 0).start()

        @pl.when(inner & (c + PASSED < chunks))
        def _():
            piece(c + PASSED, out_of, across, 1).wait_recv()
            piece(c + PASSED, out_of, across, 1).start()

        @pl.when(outer & (c < (chunks - FIRST) // 2))
        def _():
            for i in range(2):
                piece(FIRST + 2 * c + i, t, in_of, 0).start()

        @pl.when(c == 1)
        def _():
            for which in range(2):
                kv_copy(0, which).wait_recv()

            @pl.when(odd)
            def _():
                for which in range(2):
                    kv_copy(1, which).start()

        @pl.when(inner & (c == 1))
        def _():
            for k in (2, 3):
                w_copy(w_outer, quarter[k], k, (sibling, t)).wait_recv()
                w_copy(w_outer, quarter[k], 4 + k, (sibling, t)).start()

        @pl.when(c == 4)
        def _():
            for which in range(2):
                kv_copy(1, which).wait_recv()

        @pl.when(c == chunks - 1)
        def _():
            lax.fori_loop(0, early, finish, 0)

        @pl.when(inner)
        def _():
            piece(c, across, across, 0).wait_recv()
            piece(c, 3 - out_of, across, 0).wait_recv()

            @pl.when(c < DIRECT)
            def _():
                piece(c, across, out_of, 3).start()
                piece(c, 3 - out_of, out_of, 4).start()

            @pl.when(c == LAG)
            def _():
                for k in range(4):
                    w_copy(w_outer, quarter[k] + 1 - 2 * core, 4 + k, (sibling, t)).wait_recv()

            lax.fori_loop(jnp.where(c <= LAG, DIRECT, c), jnp.where(c < LAG, DIRECT, c + 1), project_outer, 0)

        @pl.when(outer & (c < DIRECT))
        def _():
            for origin in (in_of, 3 - in_of, 3 - t):
                piece(c, origin, in_of, 0).wait_recv()

        @pl.when(inner | (c < DIRECT))
        def _():
            project_own(c)

        @pl.when(odd & (c == 0))
        def _():
            for which in range(2):
                kv_skip(which).start()

        @pl.when(outer & (c >= DIRECT))
        def _():
            take(c)

        lax.fori_loop(bound(c), bound(c + 1), item, 0)

        @pl.when(c >= paired)
        def _():
            weigh_last(c)

        return 0

    lax.fori_loop(0, chunks, step, 0)
    lax.fori_loop(early, chunks, finish, 0)

    for which in range(2):
        kv_copy(0, which).wait_send()

    @pl.when(odd)
    def _():
        for which in range(2):
            kv_copy(1, which).wait_send()
            kv_skip(which).wait_send()

    def close_stats(c, _):
        for k in (1, 2, 3):
            stat_copy(c, k).wait_send()
        return 0

    lax.fori_loop(0, chunks, close_stats, 0)

    @pl.when(outer)
    def _():
        def close(c, _):
            piece(c, t, in_of, 0).wait_send()
            return 0

        lax.fori_loop(0, chunks, close, 0)
        w_copy(w_own, place, 0, (s, in_of)).wait_send()

    @pl.when(inner)
    def _():
        def close(c, _):
            piece(c, t, across, 0).wait_send()
            piece(c, out_of, across, 1).wait_send()
            return 0

        def close_direct(c, _):
            piece(c, t, out_of, 2).wait_send()
            piece(c, across, out_of, 3).wait_send()
            piece(c, 3 - out_of, out_of, 4).wait_send()
            return 0

        def close_projected(c, _):
            for which in range(2):
                qg_copy(c, which, out_of).wait_send()
            return 0

        lax.fori_loop(0, chunks, close, 0)
        lax.fori_loop(0, DIRECT, close_direct, 0)
        lax.fori_loop(DIRECT, chunks, close_projected, 0)
        w_copy(w_outer, place, 1, (base + beside, t)).wait_send()
        w_copy(w_outer, place, 2, (base + over, t)).wait_send()
        w_copy(w_outer, beside, 3, (base + over, t)).wait_send()
        for k in range(4):
            w_copy(w_outer, quarter[k], 4 + k, (sibling, t)).wait_send()


def body(
    n_seq, targets, w_query, w_gate, norm_gain, hist_keys, hist_values, user_offset, user_length, target_user
):
    rows_total, width = targets.shape
    depth, local = w_query.shape
    hist_rows = hist_keys.shape[0]
    chunks = rows_total // R
    anywhere = pl.BlockSpec(memory_space=pltpu.HBM)
    vmem = pl.BlockSpec(memory_space=pltpu.VMEM)
    smem = pl.BlockSpec(memory_space=pltpu.SMEM)
    dma = pltpu.SemaphoreType.DMA
    bf16, f32 = jnp.bfloat16, jnp.float32
    flops = 4 * rows_total * (1.5 * depth * local + (SPAN + 1) * hist_rows * local)
    return pl.pallas_call(
        functools.partial(kernel, n_seq),
        out_shape=jax.ShapeDtypeStruct((rows_total, local), bf16),
        in_specs=[anywhere, anywhere, anywhere, vmem, anywhere, anywhere, smem, smem, vmem],
        out_specs=vmem,
        scratch_shapes=[
            pltpu.VMEM((4, rows_total, width), bf16),
            pltpu.VMEM((2, depth, local), bf16),
            pltpu.VMEM((2, depth, local), bf16),
            pltpu.VMEM((SPAN + 1, 2, hist_rows, local), bf16),
            pltpu.VMEM((2, rows_total, local), bf16),
            pltpu.VMEM((2, rows_total, local), bf16),
            pltpu.VMEM((rows_total, local), f32),
            pltpu.VMEM((rows_total, local), f32),
            pltpu.VMEM((rows_total, R), f32),
            pltpu.VMEM((rows_total, R), f32),
            pltpu.VMEM((4, chunks, 8, R), f32),
            dma((5,)),
            dma((chunks, 5)),
            dma((chunks, 4)),
            dma((8,)),
            dma((GROUP,)),
            dma((SPAN + 1, 2)),
            dma((SPAN, 2)),
            dma((chunks, 2)),
            dma((chunks, 2)),
            dma((chunks, 4)),
            dma((chunks, 4)),
        ],
        compiler_params=pltpu.CompilerParams(
            collective_id=0, has_side_effects=True, vmem_limit_bytes=60 * 1024 * 1024
        ),
        cost_estimate=pl.CostEstimate(flops=int(flops), bytes_accessed=5 * 1024 * 1024, transcendentals=0),
    )(
        targets,
        w_query,
        w_gate,
        norm_gain.reshape(1, local),
        hist_keys,
        hist_values,
        user_offset,
        user_length,
        target_user.reshape(chunks, R),
    )


def solution(mesh):
    return jax.shard_map(
        functools.partial(body, mesh.shape["seq"]),
        mesh=mesh,
        in_specs=(
            P("seq", "tp"),
            P(None, "tp"),
            P(None, "tp"),
            P("tp"),
            P("seq", "tp"),
            P("seq", "tp"),
            P("seq"),
            P("seq"),
            P("seq"),
        ),
        out_specs=P("seq", "tp"),
        check_vma=False,
    )
```

```python
import functools

import jax
import jax.numpy as jnp
from jax import lax
from jax.experimental import pallas as pl
from jax.experimental.pallas import tpu as pltpu
from jax.sharding import PartitionSpec as P

HDIM = 128
SPAN = 2
HQ = 1024
R = 128
BLOCK = 256
AHEAD = 4
PASSED = 3
DIRECT = 4
LAG = 5
FIRST = 4
GROUP = 8
MESH = pl.DeviceIdType.MESH


def kernel(
    n_seq,
    targets,
    w_query,
    w_gate,
    gain,
    hist_keys,
    hist_values,
    user_offset,
    user_length,
    target_user,
    out,
    pieces,
    w_own,
    w_outer,
    kv,
    qg,
    qg_outer,
    gate,
    att,
    mids,
    halves,
    stats,
    load_sem,
    piece_send,
    piece_recv,
    w_send,
    w_recv,
    kv_send,
    kv_recv,
    qg_send,
    qg_recv,
    stat_send,
    stat_recv,
):
    rows_total, width = targets.shape
    local = w_query.shape[1]
    heads = local // HDIM
    hist_rows = hist_keys.shape[0]
    users = user_offset.shape[0]
    chunks = rows_total // R
    s = lax.axis_index("seq")
    t = lax.axis_index("tp")
    inner = (t == 1) | (t == 2)
    outer = (t == 0) | (t == 3)
    out_of = 3 * (t - 1)
    across = 3 - t
    in_of = 1 + t // 3
    behind = lax.rem(s + n_seq - 1, n_seq)
    ahead = lax.rem(s + 1, n_seq)
    behind2 = lax.rem(s + n_seq - 2, n_seq)
    ahead2 = lax.rem(s + 2, n_seq)
    odd = lax.rem(s, 2) == 1
    place = lax.rem(s, GROUP)
    base = s - place
    core = lax.rem(place, 2)
    sibling = base + place + 1 - 2 * core
    w_rows = w_query.shape[0] // GROUP

    def rows(c):
        return pl.ds(pl.multiple_of(c * R, R), R)

    def remote(src, dst, send, recv, device):
        return pltpu.make_async_remote_copy(
            src_ref=src, dst_ref=dst, send_sem=send, recv_sem=recv, device_id=device, device_id_type=MESH
        )

    def piece(c, origin, to, which):
        ref = pieces.at[origin, rows(c)]
        return remote(ref, ref, piece_send.at[c, which], piece_recv.at[c, origin], (s, to))

    def w_slice(buffer, j):
        return buffer.at[:, pl.ds(pl.multiple_of(j * w_rows, w_rows), w_rows)]

    def w_copy(src, j, which, device):
        return remote(w_slice(src, j), w_slice(w_outer, j), w_send.at[which], w_recv.at[j], device)

    bit = lax.rem(place // 2, 2)
    beside = place + 2 - 4 * bit
    over = place + 4 - 8 * (place // 4)
    corner = over + 2 - 4 * bit
    quarter = (place, beside, over, corner)

    def kv_copy(hop, which):
        return remote(
            kv.at[hop, which], kv.at[hop + 1, which], kv_send.at[hop, which], kv_recv.at[hop, which], (behind, t)
        )

    def kv_skip(which):
        return remote(kv.at[0, which], kv.at[2, which], kv_send.at[2, which], kv_recv.at[1, which], (behind2, t))

    def qg_copy(c, which, to):
        return remote(
            qg_outer.at[which, rows(c)], qg.at[which, rows(c)], qg_send.at[c, which], qg_recv.at[c, which], (s, to)
        )

    def stat_copy(c, k):
        peer = lax.rem(t + k, 4)
        return remote(stats.at[t, c], stats.at[t, c], stat_send.at[c, k], stat_recv.at[c, t], (s, peer))

    def stat_arrival(c, k):
        peer = lax.rem(t + k, 4)
        return remote(stats.at[peer, c], stats.at[peer, c], stat_send.at[c, k], stat_recv.at[c, peer], (s, peer))

    loads = [
        pltpu.make_async_copy(src, dst, load_sem.at[i])
        for i, (src, dst) in enumerate(
            [
                (targets, pieces.at[t]),
                (hist_keys, kv.at[0, 0]),
                (hist_values, kv.at[0, 1]),
                (w_query, w_own.at[0]),
                (w_gate, w_own.at[1]),
            ]
        )
    ]
    for load in loads:
        load.start()

    barrier = pltpu.get_barrier_semaphore()
    partners = [(s, lax.rem(t + k, 4)) for k in (1, 2, 3)]
    partners += [(behind, t), (ahead, t), (behind2, t), (ahead2, t)]
    partners += [(base + beside, t), (base + over, t)]
    partners += [(sibling, t)]
    for device in partners:
        pl.semaphore_signal(barrier, inc=1, device_id=device, device_id_type=MESH)
    pl.semaphore_wait(barrier, len(partners))

    loads[0].wait()

    @pl.when(outer)
    def _():
        for c in range(FIRST):
            piece(c, t, in_of, 0).start()

    @pl.when(inner)
    def _():
        for c in range(AHEAD):
            piece(c, t, across, 0).start()
        for c in range(DIRECT):
            piece(c, t, out_of, 2).start()

    for which in range(2):
        loads[1 + which].wait()
        kv_copy(0, which).start()

    @pl.when(odd)
    def _():
        for which in range(2):
            kv_skip(which).start()

    loads[3].wait()
    loads[4].wait()

    @pl.when(outer)
    def _():
        w_copy(w_own, place, 0, (s, in_of)).start()

    att[...] = jnp.zeros(att.shape, jnp.float32)

    mine = target_user[...] - s * users
    start_of = jnp.zeros(mine.shape, jnp.float32)
    length_of = jnp.zeros(mine.shape, jnp.float32)
    for u in range(users):
        match = mine == u
        start_of = jnp.where(match, (user_offset[u] - s * hist_rows).astype(jnp.float32), start_of)
        length_of = jnp.where(match, user_length[u].astype(jnp.float32), length_of)
    half_of = (length_of - 1.0) * 0.5
    mid_of = start_of + half_of
    for c in range(chunks):
        mids[c * R : (c + 1) * R, :] = jnp.broadcast_to(mid_of[c : c + 1, :], (R, R)).T
        halves[c * R : (c + 1) * R, :] = jnp.broadcast_to(half_of[c : c + 1, :], (R, R)).T

    def project(c, weights):
        sums = [jnp.zeros((R, local), jnp.float32)] * 2
        for o in range(4):
            x = pieces[o, rows(c)]
            for i in range(2):
                sums[i] = sums[i] + jnp.dot(
                    x, weights[i, o * width : (o + 1) * width, :], preferred_element_type=jnp.float32
                )
        half = sums[1] * 0.5
        return sums[0].astype(jnp.bfloat16), half + half * jnp.tanh(half)

    def weigh(c, count, hop):
        here = pl.ds(pl.multiple_of(c * R, R), count * R)
        query = qg[0, here]
        repeat = BLOCK // R
        mid = jnp.concatenate([mids[here]] * repeat, axis=1)
        half_width = jnp.concatenate([halves[here]] * repeat, axis=1)
        lanes = lax.broadcasted_iota(jnp.int32, (1, BLOCK), 1)
        sums = [att[here, h * HDIM : (h + 1) * HDIM] for h in range(heads)]
        for b in range(hist_rows // BLOCK):
            places = (lanes + (hop * hist_rows + b * BLOCK)).astype(jnp.float32)
            inside = jnp.abs(places - mid) <= half_width
            for h in range(heads):
                cols = slice(h * HDIM, (h + 1) * HDIM)
                keys = kv[hop, 0, b * BLOCK : (b + 1) * BLOCK, cols]
                values = kv[hop, 1, b * BLOCK : (b + 1) * BLOCK, cols]
                score = lax.dot_general(
                    query[:, cols], keys, (((1,), (1,)), ((), ())), preferred_element_type=jnp.float32
                )
                x = score * (0.5 * HDIM**-0.5)
                weight = jnp.where(inside, x + x * jnp.tanh(x), 0.0).astype(jnp.bfloat16)
                sums[h] = sums[h] + jnp.dot(weight, values, preferred_element_type=jnp.float32)
        for h in range(heads):
            att[here, h * HDIM : (h + 1) * HDIM] = sums[h]

    def send_stats(c):
        attended = att[rows(c)]
        first = jnp.sum(attended, axis=1, keepdims=True)
        second = jnp.sum(attended * attended, axis=1, keepdims=True)
        lane = lax.broadcasted_iota(jnp.int32, (R, R), 1)
        both = jnp.where(lane == 0, first, jnp.where(lane == 1, second, 0.0))
        stats[t, c] = both.T[:8]
        for k in (1, 2, 3):
            stat_copy(c, k).start()

    def weigh_pair(p, hop):
        weigh(2 * p, 2, hop)

        @pl.when(hop == SPAN)
        def _():
            send_stats(2 * p)
            send_stats(2 * p + 1)

    def weigh_last(c):
        def step(hop, _):
            weigh(c, 1, hop)
            return 0

        lax.fori_loop(0, SPAN + 1, step, 0)
        send_stats(c)

    def finish(c, _):
        total = stats[t, c]
        for k in (1, 2, 3):
            stat_arrival(c, k).wait_recv()
            total = total + stats[lax.rem(t + k, 4), c]
        columns = jnp.concatenate([total, jnp.zeros((R - 8, R), jnp.float32)], axis=0).T
        mean = columns[:, 0:1] * (1.0 / HQ)
        var = columns[:, 1:2] * (1.0 / HQ) - mean * mean
        normed = (att[rows(c)] - mean) * lax.rsqrt(var + 1e-05)
        out[rows(c)] = (normed * gain[...] * gate[rows(c)]).astype(jnp.bfloat16)
        return 0

    early = chunks // 2
    paired = chunks - 2

    def take(c):
        for which in range(2):
            qg_copy(c, which, in_of).wait_recv()
        gate[rows(c)] = qg[1, rows(c)].astype(jnp.float32)

    def project_own(c):
        query, gated = project(c, w_own)
        qg[0, rows(c)] = query
        gate[rows(c)] = gated

    def project_outer(c, _):
        query, gated = project(c, w_outer)
        qg_outer[0, rows(c)] = query
        qg_outer[1, rows(c)] = gated.astype(jnp.bfloat16)
        for which in range(2):
            qg_copy(c, which, out_of).start()
        return 0

    @pl.when(inner)
    def _():
        for c in range(PASSED):
            piece(c, out_of, across, 1).wait_recv()
            piece(c, out_of, across, 1).start()

    def item(i, _):
        p = jnp.where(i >= 6, 2, jnp.where((i == 2) | (i == 3) | (i == 5), 1, 0))
        hop = jnp.where(i >= 6, i - 6, jnp.where(i >= 4, 2, i % 2))
        weigh_pair(p, hop)
        return 0

    def bound(c):
        last = jnp.where(c == 4, 4, jnp.where(c == 5, 6, 9))
        return jnp.where(c <= 1, 0, jnp.where(c <= 3, c - 1, last))

    def step(c, _):
        @pl.when(inner & (c + AHEAD < chunks))
        def _():
            piece(c + AHEAD, t, across, 0).start()

        @pl.when(inner & (c + PASSED < chunks))
        def _():
            piece(c + PASSED, out_of, across, 1).wait_recv()
            piece(c + PASSED, out_of, across, 1).start()

        @pl.when(outer & (c < (chunks - FIRST) // 2))
        def _():
            for i in range(2):
                piece(FIRST + 2 * c + i, t, in_of, 0).start()

        @pl.when(c == 2)
        def _():
            for which in range(2):
                kv_copy(0, which).wait_recv()

            @pl.when(odd)
            def _():
                for which in range(2):
                    kv_copy(1, which).start()

        @pl.when(inner & (c == 1))
        def _():
            w_copy(w_outer, place, 0, (s, t)).wait_recv()
            w_copy(w_outer, place, 1, (base + beside, t)).start()
            w_copy(w_outer, place, 4, (sibling, t)).start()

        @pl.when(inner & (c == 2))
        def _():
            w_copy(w_outer, beside, 1, (base + beside, t)).wait_recv()
            w_copy(w_outer, place, 2, (base + over, t)).start()
            w_copy(w_outer, beside, 3, (base + over, t)).start()
            w_copy(w_outer, beside, 5, (sibling, t)).start()

        @pl.when(inner & (c == LAG - 1))
        def _():
            for k in (2, 3):
                w_copy(w_outer, quarter[k], k, (sibling, t)).wait_recv()
                w_copy(w_outer, quarter[k], 4 + k, (sibling, t)).start()

        @pl.when(c == 4)
        def _():
            for which in range(2):
                kv_copy(1, which).wait_recv()

        @pl.when(c == chunks - 1)
        def _():
            lax.fori_loop(0, early, finish, 0)

        @pl.when(inner)
        def _():
            piece(c, across, across, 0).wait_recv()
            piece(c, 3 - out_of, across, 0).wait_recv()

            @pl.when(c < DIRECT)
            def _():
                piece(c, across, out_of, 3).start()
                piece(c, 3 - out_of, out_of, 4).start()

            @pl.when(c == LAG)
            def _():
                for k in range(4):
                    w_copy(w_outer, quarter[k] + 1 - 2 * core, 4 + k, (sibling, t)).wait_recv()

            lax.fori_loop(jnp.where(c <= LAG, DIRECT, c), jnp.where(c < LAG, DIRECT, c + 1), project_outer, 0)

        @pl.when(outer & (c < DIRECT))
        def _():
            for origin in (in_of, 3 - in_of, 3 - t):
                piece(c, origin, in_of, 0).wait_recv()

        @pl.when(inner | (c < DIRECT))
        def _():
            project_own(c)

        @pl.when(outer & (c >= DIRECT))
        def _():
            take(c)

        lax.fori_loop(bound(c), bound(c + 1), item, 0)

        @pl.when(c >= paired)
        def _():
            weigh_last(c)

        return 0

    lax.fori_loop(0, chunks, step, 0)
    lax.fori_loop(early, chunks, finish, 0)

    for which in range(2):
        kv_copy(0, which).wait_send()

    @pl.when(odd)
    def _():
        for which in range(2):
            kv_copy(1, which).wait_send()
            kv_skip(which).wait_send()

    def close_stats(c, _):
        for k in (1, 2, 3):
            stat_copy(c, k).wait_send()
        return 0

    lax.fori_loop(0, chunks, close_stats, 0)

    @pl.when(outer)
    def _():
        def close(c, _):
            piece(c, t, in_of, 0).wait_send()
            return 0

        lax.fori_loop(0, chunks, close, 0)
        w_copy(w_own, place, 0, (s, in_of)).wait_send()

    @pl.when(inner)
    def _():
        def close(c, _):
            piece(c, t, across, 0).wait_send()
            piece(c, out_of, across, 1).wait_send()
            return 0

        def close_direct(c, _):
            piece(c, t, out_of, 2).wait_send()
            piece(c, across, out_of, 3).wait_send()
            piece(c, 3 - out_of, out_of, 4).wait_send()
            return 0

        def close_projected(c, _):
            for which in range(2):
                qg_copy(c, which, out_of).wait_send()
            return 0

        lax.fori_loop(0, chunks, close, 0)
        lax.fori_loop(0, DIRECT, close_direct, 0)
        lax.fori_loop(DIRECT, chunks, close_projected, 0)
        w_copy(w_outer, place, 1, (base + beside, t)).wait_send()
        w_copy(w_outer, place, 2, (base + over, t)).wait_send()
        w_copy(w_outer, beside, 3, (base + over, t)).wait_send()
        for k in range(4):
            w_copy(w_outer, quarter[k], 4 + k, (sibling, t)).wait_send()


def body(
    n_seq, targets, w_query, w_gate, norm_gain, hist_keys, hist_values, user_offset, user_length, target_user
):
    rows_total, width = targets.shape
    depth, local = w_query.shape
    hist_rows = hist_keys.shape[0]
    chunks = rows_total // R
    anywhere = pl.BlockSpec(memory_space=pltpu.HBM)
    vmem = pl.BlockSpec(memory_space=pltpu.VMEM)
    smem = pl.BlockSpec(memory_space=pltpu.SMEM)
    dma = pltpu.SemaphoreType.DMA
    bf16, f32 = jnp.bfloat16, jnp.float32
    flops = 4 * rows_total * (1.5 * depth * local + (SPAN + 1) * hist_rows * local)
    return pl.pallas_call(
        functools.partial(kernel, n_seq),
        out_shape=jax.ShapeDtypeStruct((rows_total, local), bf16),
        in_specs=[anywhere, anywhere, anywhere, vmem, anywhere, anywhere, smem, smem, vmem],
        out_specs=vmem,
        scratch_shapes=[
            pltpu.VMEM((4, rows_total, width), bf16),
            pltpu.VMEM((2, depth, local), bf16),
            pltpu.VMEM((2, depth, local), bf16),
            pltpu.VMEM((SPAN + 1, 2, hist_rows, local), bf16),
            pltpu.VMEM((2, rows_total, local), bf16),
            pltpu.VMEM((2, rows_total, local), bf16),
            pltpu.VMEM((rows_total, local), f32),
            pltpu.VMEM((rows_total, local), f32),
            pltpu.VMEM((rows_total, R), f32),
            pltpu.VMEM((rows_total, R), f32),
            pltpu.VMEM((4, chunks, 8, R), f32),
            dma((5,)),
            dma((chunks, 5)),
            dma((chunks, 4)),
            dma((8,)),
            dma((GROUP,)),
            dma((SPAN + 1, 2)),
            dma((SPAN, 2)),
            dma((chunks, 2)),
            dma((chunks, 2)),
            dma((chunks, 4)),
            dma((chunks, 4)),
        ],
        compiler_params=pltpu.CompilerParams(
            collective_id=0, has_side_effects=True, vmem_limit_bytes=60 * 1024 * 1024
        ),
        cost_estimate=pl.CostEstimate(flops=int(flops), bytes_accessed=5 * 1024 * 1024, transcendentals=0),
    )(
        targets,
        w_query,
        w_gate,
        norm_gain.reshape(1, local),
        hist_keys,
        hist_values,
        user_offset,
        user_length,
        target_user.reshape(chunks, R),
    )


def solution(mesh):
    return jax.shard_map(
        functools.partial(body, mesh.shape["seq"]),
        mesh=mesh,
        in_specs=(
            P("seq", "tp"),
            P(None, "tp"),
            P(None, "tp"),
            P("tp"),
            P("seq", "tp"),
            P("seq", "tp"),
            P("seq"),
            P("seq"),
            P("seq"),
        ),
        out_specs=P("seq", "tp"),
        check_vma=False,
    )
```

```python
import functools

import jax
import jax.numpy as jnp
from jax import lax
from jax.experimental import pallas as pl
from jax.experimental.pallas import tpu as pltpu
from jax.sharding import PartitionSpec as P

HDIM = 128
SPAN = 2
HQ = 1024
R = 128
BLOCK = 256
AHEAD = 4
PASSED = 2
DIRECT = 3
LAG = 4
FIRST = 4
GROUP = 8
MESH = pl.DeviceIdType.MESH


def kernel(
    n_seq,
    targets,
    w_query,
    w_gate,
    gain,
    hist_keys,
    hist_values,
    user_offset,
    user_length,
    target_user,
    out,
    pieces,
    w_own,
    w_outer,
    kv,
    qg,
    qg_outer,
    gate,
    att,
    mids,
    halves,
    stats,
    load_sem,
    piece_send,
    piece_recv,
    w_send,
    w_recv,
    kv_send,
    kv_recv,
    qg_send,
    qg_recv,
    stat_send,
    stat_recv,
):
    rows_total, width = targets.shape
    local = w_query.shape[1]
    heads = local // HDIM
    hist_rows = hist_keys.shape[0]
    users = user_offset.shape[0]
    chunks = rows_total // R
    s = lax.axis_index("seq")
    t = lax.axis_index("tp")
    inner = (t == 1) | (t == 2)
    outer = (t == 0) | (t == 3)
    out_of = 3 * (t - 1)
    across = 3 - t
    in_of = 1 + t // 3
    behind = lax.rem(s + n_seq - 1, n_seq)
    ahead = lax.rem(s + 1, n_seq)
    behind2 = lax.rem(s + n_seq - 2, n_seq)
    ahead2 = lax.rem(s + 2, n_seq)
    odd = lax.rem(s, 2) == 1
    place = lax.rem(s, GROUP)
    base = s - place
    core = lax.rem(place, 2)
    sibling = base + place + 1 - 2 * core
    w_rows = w_query.shape[0] // GROUP

    def rows(c):
        return pl.ds(pl.multiple_of(c * R, R), R)

    def remote(src, dst, send, recv, device):
        return pltpu.make_async_remote_copy(
            src_ref=src, dst_ref=dst, send_sem=send, recv_sem=recv, device_id=device, device_id_type=MESH
        )

    def piece(c, origin, to, which):
        ref = pieces.at[origin, rows(c)]
        return remote(ref, ref, piece_send.at[c, which], piece_recv.at[c, origin], (s, to))

    def w_slice(buffer, j):
        return buffer.at[:, pl.ds(pl.multiple_of(j * w_rows, w_rows), w_rows)]

    def w_copy(src, j, which, device):
        return remote(w_slice(src, j), w_slice(w_outer, j), w_send.at[which], w_recv.at[j], device)

    bit = lax.rem(place // 2, 2)
    beside = place + 2 - 4 * bit
    over = place + 4 - 8 * (place // 4)
    corner = over + 2 - 4 * bit
    quarter = (place, beside, over, corner)

    def kv_copy(hop, which):
        return remote(
            kv.at[hop, which], kv.at[hop + 1, which], kv_send.at[hop, which], kv_recv.at[hop, which], (behind, t)
        )

    def kv_skip(which):
        return remote(kv.at[0, which], kv.at[2, which], kv_send.at[2, which], kv_recv.at[1, which], (behind2, t))

    def qg_copy(c, which, to):
        return remote(
            qg_outer.at[which, rows(c)], qg.at[which, rows(c)], qg_send.at[c, which], qg_recv.at[c, which], (s, to)
        )

    def stat_copy(c, k):
        peer = lax.rem(t + k, 4)
        return remote(stats.at[t, c], stats.at[t, c], stat_send.at[c, k], stat_recv.at[c, t], (s, peer))

    def stat_arrival(c, k):
        peer = lax.rem(t + k, 4)
        return remote(stats.at[peer, c], stats.at[peer, c], stat_send.at[c, k], stat_recv.at[c, peer], (s, peer))

    loads = [
        pltpu.make_async_copy(src, dst, load_sem.at[i])
        for i, (src, dst) in enumerate(
            [
                (targets, pieces.at[t]),
                (hist_keys, kv.at[0, 0]),
                (hist_values, kv.at[0, 1]),
                (w_query, w_own.at[0]),
                (w_gate, w_own.at[1]),
            ]
        )
    ]
    for load in loads:
        load.start()

    barrier = pltpu.get_barrier_semaphore()
    partners = [(s, lax.rem(t + k, 4)) for k in (1, 2, 3)]
    partners += [(behind, t), (ahead, t), (behind2, t), (ahead2, t)]
    partners += [(base + beside, t), (base + over, t)]
    partners += [(sibling, t)]
    for device in partners:
        pl.semaphore_signal(barrier, inc=1, device_id=device, device_id_type=MESH)
    pl.semaphore_wait(barrier, len(partners))

    loads[0].wait()

    @pl.when(outer)
    def _():
        piece(0, t, in_of, 0).start()
        loads[3].wait()
        loads[4].wait()
        w_copy(w_own, place, 0, (s, in_of)).start()
        for c in range(1, FIRST):
            piece(c, t, in_of, 0).start()

    @pl.when(inner)
    def _():
        for c in range(AHEAD):
            piece(c, t, across, 0).start()
        for c in range(DIRECT):
            piece(c, t, out_of, 2).start()

    for which in range(2):
        loads[1 + which].wait()
        kv_copy(0, which).start()

    @pl.when(odd)
    def _():
        for which in range(2):
            kv_skip(which).start()

    @pl.when(inner)
    def _():
        loads[3].wait()
        loads[4].wait()

    att[...] = jnp.zeros(att.shape, jnp.float32)

    mine = target_user[...] - s * users
    start_of = jnp.zeros(mine.shape, jnp.float32)
    length_of = jnp.zeros(mine.shape, jnp.float32)
    for u in range(users):
        match = mine == u
        start_of = jnp.where(match, (user_offset[u] - s * hist_rows).astype(jnp.float32), start_of)
        length_of = jnp.where(match, user_length[u].astype(jnp.float32), length_of)
    half_of = (length_of - 1.0) * 0.5
    mid_of = start_of + half_of
    for c in range(chunks):
        mids[c * R : (c + 1) * R, :] = jnp.broadcast_to(mid_of[c : c + 1, :], (R, R)).T
        halves[c * R : (c + 1) * R, :] = jnp.broadcast_to(half_of[c : c + 1, :], (R, R)).T

    def project(c, weights):
        sums = [jnp.zeros((R, local), jnp.float32)] * 2
        for o in range(4):
            x = pieces[o, rows(c)]
            for i in range(2):
                sums[i] = sums[i] + jnp.dot(
                    x, weights[i, o * width : (o + 1) * width, :], preferred_element_type=jnp.float32
                )
        half = sums[1] * 0.5
        return sums[0].astype(jnp.bfloat16), half + half * jnp.tanh(half)

    def weigh(c, count, hop):
        here = pl.ds(pl.multiple_of(c * R, R), count * R)
        query = qg[0, here]
        repeat = BLOCK // R
        mid = jnp.concatenate([mids[here]] * repeat, axis=1)
        half_width = jnp.concatenate([halves[here]] * repeat, axis=1)
        lanes = lax.broadcasted_iota(jnp.int32, (1, BLOCK), 1)
        sums = [att[here, h * HDIM : (h + 1) * HDIM] for h in range(heads)]
        for b in range(hist_rows // BLOCK):
            places = (lanes + (hop * hist_rows + b * BLOCK)).astype(jnp.float32)
            inside = jnp.abs(places - mid) <= half_width
            for h in range(heads):
                cols = slice(h * HDIM, (h + 1) * HDIM)
                keys = kv[hop, 0, b * BLOCK : (b + 1) * BLOCK, cols]
                values = kv[hop, 1, b * BLOCK : (b + 1) * BLOCK, cols]
                score = lax.dot_general(
                    query[:, cols], keys, (((1,), (1,)), ((), ())), preferred_element_type=jnp.float32
                )
                x = score * (0.5 * HDIM**-0.5)
                weight = jnp.where(inside, x + x * jnp.tanh(x), 0.0).astype(jnp.bfloat16)
                sums[h] = sums[h] + jnp.dot(weight, values, preferred_element_type=jnp.float32)
        for h in range(heads):
            att[here, h * HDIM : (h + 1) * HDIM] = sums[h]

    def send_stats(c):
        attended = att[rows(c)]
        first = jnp.sum(attended, axis=1, keepdims=True)
        second = jnp.sum(attended * attended, axis=1, keepdims=True)
        lane = lax.broadcasted_iota(jnp.int32, (R, R), 1)
        both = jnp.where(lane == 0, first, jnp.where(lane == 1, second, 0.0))
        stats[t, c] = both.T[:8]
        for k in (1, 2, 3):
            stat_copy(c, k).start()

    def weigh_pair(p, hop):
        weigh(2 * p, 2, hop)

        @pl.when(hop == SPAN)
        def _():
            send_stats(2 * p)
            send_stats(2 * p + 1)

    def weigh_last(c):
        def step(hop, _):
            weigh(c, 1, hop)
            return 0

        lax.fori_loop(0, SPAN + 1, step, 0)
        send_stats(c)

    def finish(c, _):
        total = stats[t, c]
        for k in (1, 2, 3):
            stat_arrival(c, k).wait_recv()
            total = total + stats[lax.rem(t + k, 4), c]
        columns = jnp.concatenate([total, jnp.zeros((R - 8, R), jnp.float32)], axis=0).T
        mean = columns[:, 0:1] * (1.0 / HQ)
        var = columns[:, 1:2] * (1.0 / HQ) - mean * mean
        normed = (att[rows(c)] - mean) * lax.rsqrt(var + 1e-05)
        out[rows(c)] = (normed * gain[...] * gate[rows(c)]).astype(jnp.bfloat16)
        return 0

    early = chunks // 2
    paired = chunks - 2

    def take(c):
        for which in range(2):
            qg_copy(c, which, in_of).wait_recv()
        gate[rows(c)] = qg[1, rows(c)].astype(jnp.float32)

    def project_own(c):
        query, gated = project(c, w_own)
        qg[0, rows(c)] = query
        gate[rows(c)] = gated

    def project_outer(c, _):
        query, gated = project(c, w_outer)
        qg_outer[0, rows(c)] = query
        qg_outer[1, rows(c)] = gated.astype(jnp.bfloat16)
        for which in range(2):
            qg_copy(c, which, out_of).start()
        return 0

    @pl.when(inner)
    def _():
        piece(0, out_of, across, 1).wait_recv()
        piece(0, out_of, across, 1).start()
        w_copy(w_outer, place, 0, (s, t)).wait_recv()
        w_copy(w_outer, place, 1, (base + beside, t)).start()
        w_copy(w_outer, place, 4, (sibling, t)).start()
        for c in range(1, PASSED):
            piece(c, out_of, across, 1).wait_recv()
            piece(c, out_of, across, 1).start()

    def item(i, _):
        weigh_pair(i // (SPAN + 1), i % (SPAN + 1))
        return 0

    def first_item(c):
        late = jnp.where(c == 4, 5, jnp.where(c == 5, 6, 9))
        return jnp.where(c <= 1, 0, jnp.where(c == 2, 1, jnp.where(c == 3, 3, late)))

    def last_item(c):
        late = jnp.where(c == 3, 5, jnp.where(c == 4, 6, 9))
        return jnp.where(c <= 2, c, late)

    def step(c, _):
        @pl.when(inner & (c + AHEAD < chunks))
        def _():
            piece(c + AHEAD, t, across, 0).start()

        @pl.when(inner & (c + PASSED < chunks))
        def _():
            piece(c + PASSED, out_of, across, 1).wait_recv()
            piece(c + PASSED, out_of, across, 1).start()

        @pl.when(outer & (c < (chunks - FIRST) // 2))
        def _():
            for i in range(2):
                piece(FIRST + 2 * c + i, t, in_of, 0).start()

        @pl.when(c == 2)
        def _():
            for which in range(2):
                kv_copy(0, which).wait_recv()

            @pl.when(odd)
            def _():
                for which in range(2):
                    kv_copy(1, which).start()

        @pl.when(inner & (c == 1))
        def _():
            w_copy(w_outer, beside, 1, (base + beside, t)).wait_recv()
            w_copy(w_outer, place, 2, (base + over, t)).start()
            w_copy(w_outer, beside, 3, (base + over, t)).start()
            w_copy(w_outer, beside, 5, (sibling, t)).start()

        @pl.when(inner & (c == LAG - 1))
        def _():
            for k in (2, 3):
                w_copy(w_outer, quarter[k], k, (sibling, t)).wait_recv()
                w_copy(w_outer, quarter[k], 4 + k, (sibling, t)).start()

        @pl.when(c == 3)
        def _():
            for which in range(2):
                kv_copy(1, which).wait_recv()
            lax.fori_loop(2, 3, item, 0)

        @pl.when(c == chunks - 1)
        def _():
            lax.fori_loop(0, early, finish, 0)

        @pl.when(inner)
        def _():
            piece(c, across, across, 0).wait_recv()
            piece(c, 3 - out_of, across, 0).wait_recv()

            @pl.when(c < DIRECT)
            def _():
                piece(c, across, out_of, 3).start()
                piece(c, 3 - out_of, out_of, 4).start()

            @pl.when(c == LAG)
            def _():
                for k in range(4):
                    w_copy(w_outer, quarter[k] + 1 - 2 * core, 4 + k, (sibling, t)).wait_recv()

            lax.fori_loop(jnp.where(c <= LAG, DIRECT, c), jnp.where(c < LAG, DIRECT, c + 1), project_outer, 0)

        @pl.when(outer & (c < DIRECT))
        def _():
            for origin in (in_of, 3 - in_of, 3 - t):
                piece(c, origin, in_of, 0).wait_recv()

        @pl.when(inner | (c < DIRECT))
        def _():
            project_own(c)

        @pl.when(outer & (c >= DIRECT))
        def _():
            take(c)

        lax.fori_loop(first_item(c), last_item(c), item, 0)

        @pl.when(c >= paired)
        def _():
            weigh_last(c)

        return 0

    lax.fori_loop(0, chunks, step, 0)
    lax.fori_loop(early, chunks, finish, 0)

    for which in range(2):
        kv_copy(0, which).wait_send()

    @pl.when(odd)
    def _():
        for which in range(2):
            kv_copy(1, which).wait_send()
            kv_skip(which).wait_send()

    def close_stats(c, _):
        for k in (1, 2, 3):
            stat_copy(c, k).wait_send()
        return 0

    lax.fori_loop(0, chunks, close_stats, 0)

    @pl.when(outer)
    def _():
        def close(c, _):
            piece(c, t, in_of, 0).wait_send()
            return 0

        lax.fori_loop(0, chunks, close, 0)
        w_copy(w_own, place, 0, (s, in_of)).wait_send()

    @pl.when(inner)
    def _():
        def close(c, _):
            piece(c, t, across, 0).wait_send()
            piece(c, out_of, across, 1).wait_send()
            return 0

        def close_direct(c, _):
            piece(c, t, out_of, 2).wait_send()
            piece(c, across, out_of, 3).wait_send()
            piece(c, 3 - out_of, out_of, 4).wait_send()
            return 0

        def close_projected(c, _):
            for which in range(2):
                qg_copy(c, which, out_of).wait_send()
            return 0

        lax.fori_loop(0, chunks, close, 0)
        lax.fori_loop(0, DIRECT, close_direct, 0)
        lax.fori_loop(DIRECT, chunks, close_projected, 0)
        w_copy(w_outer, place, 1, (base + beside, t)).wait_send()
        w_copy(w_outer, place, 2, (base + over, t)).wait_send()
        w_copy(w_outer, beside, 3, (base + over, t)).wait_send()
        for k in range(4):
            w_copy(w_outer, quarter[k], 4 + k, (sibling, t)).wait_send()


def body(
    n_seq, targets, w_query, w_gate, norm_gain, hist_keys, hist_values, user_offset, user_length, target_user
):
    rows_total, width = targets.shape
    depth, local = w_query.shape
    hist_rows = hist_keys.shape[0]
    chunks = rows_total // R
    anywhere = pl.BlockSpec(memory_space=pltpu.HBM)
    vmem = pl.BlockSpec(memory_space=pltpu.VMEM)
    smem = pl.BlockSpec(memory_space=pltpu.SMEM)
    dma = pltpu.SemaphoreType.DMA
    bf16, f32 = jnp.bfloat16, jnp.float32
    flops = 4 * rows_total * (1.5 * depth * local + (SPAN + 1) * hist_rows * local)
    return pl.pallas_call(
        functools.partial(kernel, n_seq),
        out_shape=jax.ShapeDtypeStruct((rows_total, local), bf16),
        in_specs=[anywhere, anywhere, anywhere, vmem, anywhere, anywhere, smem, smem, vmem],
        out_specs=vmem,
        scratch_shapes=[
            pltpu.VMEM((4, rows_total, width), bf16),
            pltpu.VMEM((2, depth, local), bf16),
            pltpu.VMEM((2, depth, local), bf16),
            pltpu.VMEM((SPAN + 1, 2, hist_rows, local), bf16),
            pltpu.VMEM((2, rows_total, local), bf16),
            pltpu.VMEM((2, rows_total, local), bf16),
            pltpu.VMEM((rows_total, local), f32),
            pltpu.VMEM((rows_total, local), f32),
            pltpu.VMEM((rows_total, R), f32),
            pltpu.VMEM((rows_total, R), f32),
            pltpu.VMEM((4, chunks, 8, R), f32),
            dma((5,)),
            dma((chunks, 5)),
            dma((chunks, 4)),
            dma((8,)),
            dma((GROUP,)),
            dma((SPAN + 1, 2)),
            dma((SPAN, 2)),
            dma((chunks, 2)),
            dma((chunks, 2)),
            dma((chunks, 4)),
            dma((chunks, 4)),
        ],
        compiler_params=pltpu.CompilerParams(
            collective_id=0, has_side_effects=True, vmem_limit_bytes=60 * 1024 * 1024
        ),
        cost_estimate=pl.CostEstimate(flops=int(flops), bytes_accessed=5 * 1024 * 1024, transcendentals=0),
    )(
        targets,
        w_query,
        w_gate,
        norm_gain.reshape(1, local),
        hist_keys,
        hist_values,
        user_offset,
        user_length,
        target_user.reshape(chunks, R),
    )


def solution(mesh):
    return jax.shard_map(
        functools.partial(body, mesh.shape["seq"]),
        mesh=mesh,
        in_specs=(
            P("seq", "tp"),
            P(None, "tp"),
            P(None, "tp"),
            P("tp"),
            P("seq", "tp"),
            P("seq", "tp"),
            P("seq"),
            P("seq"),
            P("seq"),
        ),
        out_specs=P("seq", "tp"),
        check_vma=False,
    )
```

```python
import functools

import jax
import jax.numpy as jnp
from jax import lax
from jax.experimental import pallas as pl
from jax.experimental.pallas import tpu as pltpu
from jax.sharding import PartitionSpec as P

HDIM = 128
SPAN = 2
HQ = 1024
R = 128
BLOCK = 256
AHEAD = 4
PASSED = 3
DIRECT = 4
LAG = 5
FIRST = 4
GROUP = 8
MESH = pl.DeviceIdType.MESH


def kernel(
    n_seq,
    targets,
    w_query,
    w_gate,
    gain,
    hist_keys,
    hist_values,
    user_offset,
    user_length,
    target_user,
    out,
    pieces,
    w_own,
    w_outer,
    kv,
    qg,
    qg_outer,
    gate,
    att,
    mids,
    halves,
    stats,
    load_sem,
    piece_send,
    piece_recv,
    w_send,
    w_recv,
    kv_send,
    kv_recv,
    qg_send,
    qg_recv,
    stat_send,
    stat_recv,
):
    rows_total, width = targets.shape
    local = w_query.shape[1]
    heads = local // HDIM
    hist_rows = hist_keys.shape[0]
    users = user_offset.shape[0]
    chunks = rows_total // R
    s = lax.axis_index("seq")
    t = lax.axis_index("tp")
    inner = (t == 1) | (t == 2)
    outer = (t == 0) | (t == 3)
    out_of = 3 * (t - 1)
    across = 3 - t
    in_of = 1 + t // 3
    behind = lax.rem(s + n_seq - 1, n_seq)
    ahead = lax.rem(s + 1, n_seq)
    behind2 = lax.rem(s + n_seq - 2, n_seq)
    ahead2 = lax.rem(s + 2, n_seq)
    odd = lax.rem(s, 2) == 1
    place = lax.rem(s, GROUP)
    base = s - place
    core = lax.rem(place, 2)
    sibling = base + place + 1 - 2 * core
    w_rows = w_query.shape[0] // GROUP

    def rows(c):
        return pl.ds(pl.multiple_of(c * R, R), R)

    def remote(src, dst, send, recv, device):
        return pltpu.make_async_remote_copy(
            src_ref=src, dst_ref=dst, send_sem=send, recv_sem=recv, device_id=device, device_id_type=MESH
        )

    def piece(c, origin, to, which):
        ref = pieces.at[origin, rows(c)]
        return remote(ref, ref, piece_send.at[c, which], piece_recv.at[c, origin], (s, to))

    def w_slice(buffer, j):
        return buffer.at[:, pl.ds(pl.multiple_of(j * w_rows, w_rows), w_rows)]

    def w_copy(src, j, which, device):
        return remote(w_slice(src, j), w_slice(w_outer, j), w_send.at[which], w_recv.at[j], device)

    bit = lax.rem(place // 2, 2)
    beside = place + 2 - 4 * bit
    over = place + 4 - 8 * (place // 4)
    corner = over + 2 - 4 * bit
    quarter = (place, beside, over, corner)

    def kv_copy(hop, which):
        return remote(
            kv.at[hop, which], kv.at[hop + 1, which], kv_send.at[hop, which], kv_recv.at[hop, which], (behind, t)
        )

    def kv_skip(which):
        return remote(kv.at[0, which], kv.at[2, which], kv_send.at[2, which], kv_recv.at[1, which], (behind2, t))

    def qg_copy(c, which, to):
        return remote(
            qg_outer.at[which, rows(c)], qg.at[which, rows(c)], qg_send.at[c, which], qg_recv.at[c, which], (s, to)
        )

    def stat_copy(c, k):
        peer = lax.rem(t + k, 4)
        return remote(stats.at[t, c], stats.at[t, c], stat_send.at[c, k], stat_recv.at[c, t], (s, peer))

    def stat_arrival(c, k):
        peer = lax.rem(t + k, 4)
        return remote(stats.at[peer, c], stats.at[peer, c], stat_send.at[c, k], stat_recv.at[c, peer], (s, peer))

    loads = [
        pltpu.make_async_copy(src, dst, load_sem.at[i])
        for i, (src, dst) in enumerate(
            [
                (targets, pieces.at[t]),
                (hist_keys, kv.at[0, 0]),
                (hist_values, kv.at[0, 1]),
                (w_query, w_own.at[0]),
                (w_gate, w_own.at[1]),
            ]
        )
    ]
    for load in loads:
        load.start()

    barrier = pltpu.get_barrier_semaphore()
    partners = [(s, lax.rem(t + k, 4)) for k in (1, 2, 3)]
    partners += [(behind, t), (ahead, t), (behind2, t), (ahead2, t)]
    partners += [(base + beside, t), (base + over, t)]
    partners += [(sibling, t)]
    for device in partners:
        pl.semaphore_signal(barrier, inc=1, device_id=device, device_id_type=MESH)
    pl.semaphore_wait(barrier, len(partners))

    loads[0].wait()

    @pl.when(outer)
    def _():
        for c in range(FIRST):
            piece(c, t, in_of, 0).start()

    @pl.when(inner)
    def _():
        for c in range(AHEAD):
            piece(c, t, across, 0).start()
        for c in range(DIRECT):
            piece(c, t, out_of, 2).start()

    for which in range(2):
        loads[1 + which].wait()
        kv_copy(0, which).start()

    @pl.when(odd)
    def _():
        for which in range(2):
            kv_skip(which).start()

    loads[3].wait()
    loads[4].wait()

    @pl.when(outer)
    def _():
        w_copy(w_own, place, 0, (s, in_of)).start()

    att[...] = jnp.zeros(att.shape, jnp.float32)

    mine = target_user[...] - s * users
    start_of = jnp.zeros(mine.shape, jnp.float32)
    length_of = jnp.zeros(mine.shape, jnp.float32)
    for u in range(users):
        match = mine == u
        start_of = jnp.where(match, (user_offset[u] - s * hist_rows).astype(jnp.float32), start_of)
        length_of = jnp.where(match, user_length[u].astype(jnp.float32), length_of)
    half_of = (length_of - 1.0) * 0.5
    mid_of = start_of + half_of
    for c in range(chunks):
        mids[c * R : (c + 1) * R, :] = jnp.broadcast_to(mid_of[c : c + 1, :], (R, R)).T
        halves[c * R : (c + 1) * R, :] = jnp.broadcast_to(half_of[c : c + 1, :], (R, R)).T

    def project(c, weights):
        sums = [jnp.zeros((R, local), jnp.float32)] * 2
        for o in range(4):
            x = pieces[o, rows(c)]
            for i in range(2):
                sums[i] = sums[i] + jnp.dot(
                    x, weights[i, o * width : (o + 1) * width, :], preferred_element_type=jnp.float32
                )
        half = sums[1] * 0.5
        return sums[0].astype(jnp.bfloat16), half + half * jnp.tanh(half)

    def weigh(c, count, hop):
        here = pl.ds(pl.multiple_of(c * R, R), count * R)
        query = qg[0, here]
        repeat = BLOCK // R
        mid = jnp.concatenate([mids[here]] * repeat, axis=1)
        half_width = jnp.concatenate([halves[here]] * repeat, axis=1)
        lanes = lax.broadcasted_iota(jnp.int32, (1, BLOCK), 1)
        sums = [att[here, h * HDIM : (h + 1) * HDIM] for h in range(heads)]
        for b in range(hist_rows // BLOCK):
            places = (lanes + (hop * hist_rows + b * BLOCK)).astype(jnp.float32)
            inside = jnp.abs(places - mid) <= half_width
            for h in range(heads):
                cols = slice(h * HDIM, (h + 1) * HDIM)
                keys = kv[hop, 0, b * BLOCK : (b + 1) * BLOCK, cols]
                values = kv[hop, 1, b * BLOCK : (b + 1) * BLOCK, cols]
                score = lax.dot_general(
                    query[:, cols], keys, (((1,), (1,)), ((), ())), preferred_element_type=jnp.float32
                )
                x = score * (0.5 * HDIM**-0.5)
                weight = jnp.where(inside, x + x * jnp.tanh(x), 0.0).astype(jnp.bfloat16)
                sums[h] = sums[h] + jnp.dot(weight, values, preferred_element_type=jnp.float32)
        for h in range(heads):
            att[here, h * HDIM : (h + 1) * HDIM] = sums[h]

    def send_stats(c):
        attended = att[rows(c)]
        first = jnp.sum(attended, axis=1, keepdims=True)
        second = jnp.sum(attended * attended, axis=1, keepdims=True)
        lane = lax.broadcasted_iota(jnp.int32, (R, R), 1)
        both = jnp.where(lane == 0, first, jnp.where(lane == 1, second, 0.0))
        stats[t, c] = both.T[:8]
        for k in (1, 2, 3):
            stat_copy(c, k).start()

    def weigh_pair(p, hop):
        weigh(2 * p, 2, hop)

        @pl.when(hop == SPAN)
        def _():
            send_stats(2 * p)
            send_stats(2 * p + 1)

    def weigh_last(c):
        def step(hop, _):
            weigh(c, 1, hop)
            return 0

        lax.fori_loop(0, SPAN + 1, step, 0)
        send_stats(c)

    def finish(c, _):
        total = stats[t, c]
        for k in (1, 2, 3):
            stat_arrival(c, k).wait_recv()
            total = total + stats[lax.rem(t + k, 4), c]
        columns = jnp.concatenate([total, jnp.zeros((R - 8, R), jnp.float32)], axis=0).T
        mean = columns[:, 0:1] * (1.0 / HQ)
        var = columns[:, 1:2] * (1.0 / HQ) - mean * mean
        normed = (att[rows(c)] - mean) * lax.rsqrt(var + 1e-05)
        out[rows(c)] = (normed * gain[...] * gate[rows(c)]).astype(jnp.bfloat16)
        return 0

    early = chunks // 2
    paired = chunks - 2

    def take(c):
        for which in range(2):
            qg_copy(c, which, in_of).wait_recv()
        gate[rows(c)] = qg[1, rows(c)].astype(jnp.float32)

    def project_own(c):
        query, gated = project(c, w_own)
        qg[0, rows(c)] = query
        gate[rows(c)] = gated

    def project_outer(c, _):
        query, gated = project(c, w_outer)
        qg_outer[0, rows(c)] = query
        qg_outer[1, rows(c)] = gated.astype(jnp.bfloat16)
        for which in range(2):
            qg_copy(c, which, out_of).start()
        return 0

    @pl.when(inner)
    def _():
        for c in range(PASSED):
            piece(c, out_of, across, 1).wait_recv()
            piece(c, out_of, across, 1).start()

    def item(i, _):
        @pl.when(i == 6)
        def _():
            for which in range(2):
                kv_copy(1, which).wait_recv()

        p = jnp.where(i >= 6, i - 6, jnp.where(i >= 4, 2, i % 2))
        hop = jnp.where(i >= 6, 2, jnp.where(i >= 4, i - 4, i // 2))
        weigh_pair(p, hop)
        return 0

    def bound(c):
        return jnp.where(c <= 1, 0, jnp.where(c <= 3, 1, jnp.where(c <= 5, 4, 9)))

    def step(c, _):
        @pl.when(inner & (c + AHEAD < chunks))
        def _():
            piece(c + AHEAD, t, across, 0).start()

        @pl.when(inner & (c + PASSED < chunks))
        def _():
            piece(c + PASSED, out_of, across, 1).wait_recv()
            piece(c + PASSED, out_of, across, 1).start()

        @pl.when(outer & (c < (chunks - FIRST) // 2))
        def _():
            for i in range(2):
                piece(FIRST + 2 * c + i, t, in_of, 0).start()

        @pl.when(inner & (c == 1))
        def _():
            w_copy(w_outer, place, 0, (s, t)).wait_recv()
            w_copy(w_outer, place, 1, (base + beside, t)).start()
            w_copy(w_outer, place, 4, (sibling, t)).start()

        @pl.when(inner & (c == 2))
        def _():
            w_copy(w_outer, beside, 1, (base + beside, t)).wait_recv()
            w_copy(w_outer, place, 2, (base + over, t)).start()
            w_copy(w_outer, beside, 3, (base + over, t)).start()
            w_copy(w_outer, beside, 5, (sibling, t)).start()

        @pl.when(inner & (c == LAG - 1))
        def _():
            for k in (2, 3):
                w_copy(w_outer, quarter[k], k, (sibling, t)).wait_recv()
                w_copy(w_outer, quarter[k], 4 + k, (sibling, t)).start()

        @pl.when(c == chunks - 1)
        def _():
            lax.fori_loop(0, early, finish, 0)

        @pl.when(inner)
        def _():
            piece(c, across, across, 0).wait_recv()
            piece(c, 3 - out_of, across, 0).wait_recv()

            @pl.when(c < DIRECT)
            def _():
                piece(c, across, out_of, 3).start()
                piece(c, 3 - out_of, out_of, 4).start()

            @pl.when(c == LAG)
            def _():
                for k in range(4):
                    w_copy(w_outer, quarter[k] + 1 - 2 * core, 4 + k, (sibling, t)).wait_recv()

            lax.fori_loop(jnp.where(c <= LAG, DIRECT, c), jnp.where(c < LAG, DIRECT, c + 1), project_outer, 0)

        @pl.when(outer & (c < DIRECT))
        def _():
            for origin in (in_of, 3 - in_of, 3 - t):
                piece(c, origin, in_of, 0).wait_recv()

        @pl.when(inner | (c < DIRECT))
        def _():
            project_own(c)

        @pl.when(outer & (c >= DIRECT))
        def _():
            take(c)

        @pl.when(c == 2)
        def _():
            for which in range(2):
                kv_copy(0, which).wait_recv()

            @pl.when(odd)
            def _():
                for which in range(2):
                    kv_copy(1, which).start()

        lax.fori_loop(bound(c), bound(c + 1), item, 0)

        @pl.when(c >= paired)
        def _():
            weigh_last(c)

        return 0

    lax.fori_loop(0, chunks, step, 0)
    lax.fori_loop(early, chunks, finish, 0)

    for which in range(2):
        kv_copy(0, which).wait_send()

    @pl.when(odd)
    def _():
        for which in range(2):
            kv_copy(1, which).wait_send()
            kv_skip(which).wait_send()

    def close_stats(c, _):
        for k in (1, 2, 3):
            stat_copy(c, k).wait_send()
        return 0

    lax.fori_loop(0, chunks, close_stats, 0)

    @pl.when(outer)
    def _():
        def close(c, _):
            piece(c, t, in_of, 0).wait_send()
            return 0

        lax.fori_loop(0, chunks, close, 0)
        w_copy(w_own, place, 0, (s, in_of)).wait_send()

    @pl.when(inner)
    def _():
        def close(c, _):
            piece(c, t, across, 0).wait_send()
            piece(c, out_of, across, 1).wait_send()
            return 0

        def close_direct(c, _):
            piece(c, t, out_of, 2).wait_send()
            piece(c, across, out_of, 3).wait_send()
            piece(c, 3 - out_of, out_of, 4).wait_send()
            return 0

        def close_projected(c, _):
            for which in range(2):
                qg_copy(c, which, out_of).wait_send()
            return 0

        lax.fori_loop(0, chunks, close, 0)
        lax.fori_loop(0, DIRECT, close_direct, 0)
        lax.fori_loop(DIRECT, chunks, close_projected, 0)
        w_copy(w_outer, place, 1, (base + beside, t)).wait_send()
        w_copy(w_outer, place, 2, (base + over, t)).wait_send()
        w_copy(w_outer, beside, 3, (base + over, t)).wait_send()
        for k in range(4):
            w_copy(w_outer, quarter[k], 4 + k, (sibling, t)).wait_send()


def body(
    n_seq, targets, w_query, w_gate, norm_gain, hist_keys, hist_values, user_offset, user_length, target_user
):
    rows_total, width = targets.shape
    depth, local = w_query.shape
    hist_rows = hist_keys.shape[0]
    chunks = rows_total // R
    anywhere = pl.BlockSpec(memory_space=pltpu.HBM)
    vmem = pl.BlockSpec(memory_space=pltpu.VMEM)
    smem = pl.BlockSpec(memory_space=pltpu.SMEM)
    dma = pltpu.SemaphoreType.DMA
    bf16, f32 = jnp.bfloat16, jnp.float32
    flops = 4 * rows_total * (1.5 * depth * local + (SPAN + 1) * hist_rows * local)
    return pl.pallas_call(
        functools.partial(kernel, n_seq),
        out_shape=jax.ShapeDtypeStruct((rows_total, local), bf16),
        in_specs=[anywhere, anywhere, anywhere, vmem, anywhere, anywhere, smem, smem, vmem],
        out_specs=vmem,
        scratch_shapes=[
            pltpu.VMEM((4, rows_total, width), bf16),
            pltpu.VMEM((2, depth, local), bf16),
            pltpu.VMEM((2, depth, local), bf16),
            pltpu.VMEM((SPAN + 1, 2, hist_rows, local), bf16),
            pltpu.VMEM((2, rows_total, local), bf16),
            pltpu.VMEM((2, rows_total, local), bf16),
            pltpu.VMEM((rows_total, local), f32),
            pltpu.VMEM((rows_total, local), f32),
            pltpu.VMEM((rows_total, R), f32),
            pltpu.VMEM((rows_total, R), f32),
            pltpu.VMEM((4, chunks, 8, R), f32),
            dma((5,)),
            dma((chunks, 5)),
            dma((chunks, 4)),
            dma((8,)),
            dma((GROUP,)),
            dma((SPAN + 1, 2)),
            dma((SPAN, 2)),
            dma((chunks, 2)),
            dma((chunks, 2)),
            dma((chunks, 4)),
            dma((chunks, 4)),
        ],
        compiler_params=pltpu.CompilerParams(
            collective_id=0, has_side_effects=True, vmem_limit_bytes=60 * 1024 * 1024
        ),
        cost_estimate=pl.CostEstimate(flops=int(flops), bytes_accessed=5 * 1024 * 1024, transcendentals=0),
    )(
        targets,
        w_query,
        w_gate,
        norm_gain.reshape(1, local),
        hist_keys,
        hist_values,
        user_offset,
        user_length,
        target_user.reshape(chunks, R),
    )


def solution(mesh):
    return jax.shard_map(
        functools.partial(body, mesh.shape["seq"]),
        mesh=mesh,
        in_specs=(
            P("seq", "tp"),
            P(None, "tp"),
            P(None, "tp"),
            P("tp"),
            P("seq", "tp"),
            P("seq", "tp"),
            P("seq"),
            P("seq"),
            P("seq"),
        ),
        out_specs=P("seq", "tp"),
        check_vma=False,
    )
```
